256 devices in a mesh: ctx: 64 (over z, x, y_lo), ch: 4 (over y_hi, core).
Axes of the slice: x: 4, y: 4 (y_hi: 2, y_lo: 2; y = y_hi * 2 + y_lo), z: 8, core: 2. Of those that a mesh axis runs over, the one named last changes fastest.
Arguments:
- inputs: float32 [4, 16384, 1024], P(None, 'ctx', 'ch'), may hold values from -6 to 6
- cotangent: float32 [4, 16384, 1024], P(None, 'ctx', 'ch'), may hold values from -6 to 6
- filters: float32 [16384, 1024], P('ctx', 'ch'), may hold values from -6 to 6
Outputs:
- input_grad: float32 [4, 16384, 1024], P(None, 'ctx', 'ch')
- filter_grad: float32 [16384, 1024], P('ctx', 'ch')
The draws below stay inside these ranges and needn't reach their ends.
All inputs are finite; a program needn't handle non-finite values.
Results may differ from the reference program's by a relative error of at most 0.0001.
Values sent between devices are 32-bit elements; how exact they have to be, the bound alone decides.
No kernel may reach another device: no remote copies, remote signals or barrier semaphores. Data moves between devices by JAX's collectives and lax.ppermute only.
A program may use at most 128 MiB of HBM per device.

```python
import math
import jax
import jax.numpy as jnp

C = 1024
SEQS = 4
SEQ_LEN = 16384


def block_scale(key, dims, shards, low, largest):
    def one(position, parts):
        steps = jax.random.uniform(jax.random.fold_in(jax.random.fold_in(key, 6), position), (parts,), jnp.float32, low / len(shards), largest / len(shards))
        return jnp.repeat(jnp.exp(steps), dims[position] // parts).reshape((-1,) + (1,) * (len(dims) - position - 1))

    loudness = one(*shards[0])
    for cut in shards[1:]:
        loudness = loudness * one(*cut)
    return loudness


def centred(stream_key, shape, spread, reach, shards=(), kind=jnp.bfloat16):
    drawn = spread * jax.random.normal(stream_key, shape, jnp.float32)
    if shards:
        drawn = drawn * block_scale(stream_key, shape, shards, -0.22, 0.18)
    return jnp.clip(drawn, -reach, reach).astype(kind)


def setup_inputs(seed: int = 0) -> dict:
    seeds = jax.random.split(jax.random.key(seed), 4)
    inputs = centred(seeds[0], (SEQS, SEQ_LEN, C), 1.0, 6.0, ((1, 64), (2, 4)), jnp.float32)
    cotangent = centred(seeds[1], (SEQS, SEQ_LEN, C), 1.0, 6.0, ((1, 64), (2, 4)), jnp.float32)
    filters = centred(seeds[2], (SEQ_LEN, C), 1.0, 6.0, ((0, 64), (1, 4)), jnp.float32)
    return dict(inputs=inputs, cotangent=cotangent, filters=filters)


def reference(inputs, cotangent, filters):
    scale = 1.0 / math.sqrt(2.0 * SEQ_LEN)
    filter_spectrum = jnp.fft.fft(filters, axis=0)
    effective = filter_spectrum + jnp.conj(filter_spectrum[:, ::-1])
    grads = []
    cross = jnp.zeros_like(filter_spectrum)
    for index in range(SEQS):
        inputs_spectrum = jnp.fft.fft(inputs[index], axis=0)
        cotangent_spectrum = jnp.fft.fft(cotangent[index], axis=0)
        input_spec = jnp.conj(effective) * cotangent_spectrum
        grads.append(jnp.real(jnp.fft.ifft(input_spec, axis=0)) * scale)
        cross = cross + cotangent_spectrum * jnp.conj(inputs_spectrum)
    filter_spec = cross + jnp.conj(cross[:, ::-1])
    filter_grad = jnp.real(jnp.fft.ifft(filter_spec, axis=0)) * scale
    input_grad = jnp.stack(grads, axis=0)
    return (input_grad.astype(jnp.float32), filter_grad.astype(jnp.float32))
```

```python
import functools
import math

import jax
import jax.numpy as jnp
import numpy as np
from jax import lax
from jax.experimental import pallas as pl
from jax.experimental.pallas import tpu as pltpu
from jax.sharding import PartitionSpec as P

BF = jnp.bfloat16
F32 = jnp.float32
ACROSS = 64
WIDTH = 256
PERIOD = ACROSS * WIDTH
HALF = 40
KEEP = ACROSS // 2 + 1
FACTOR = 1.0 / (PERIOD * math.sqrt(2.0 * PERIOD))
VMEM = 48 * 1024 * 1024


def two_parts(table):
    high = np.asarray(table, np.float32).astype(jnp.bfloat16)
    low = (table - high.astype(np.float64)).astype(np.float32).astype(jnp.bfloat16)
    return high, low


def tables():
    p = np.arange(HALF)
    i = np.arange(ACROSS)
    keep = (p < KEEP).astype(np.float64)
    angle = 2.0 * np.pi * (np.outer(p, i) % ACROSS) / ACROSS
    cos, sin = np.cos(angle) * keep[:, None], np.sin(angle) * keep[:, None]
    high, low = two_parts(np.concatenate([cos, -sin], 0))
    across = np.concatenate([high, low, high], 1)
    weight = np.where((p == 0) | (p == KEEP - 1), 1.0, 2.0) * keep * FACTOR
    back = np.concatenate([cos * weight[:, None], sin * weight[:, None]], 0).T
    high, low = two_parts(back)
    back = np.concatenate([high, low, high], 1)
    j = np.arange(WIDTH)
    turn = 2.0 * np.pi * np.outer(p, j) / PERIOD
    twiddle = np.stack([np.cos(turn), np.sin(turn)]).astype(np.float32)
    spin = 2.0 * np.pi * (np.outer(j, j) % WIDTH) / WIDTH
    c, s = np.cos(spin), np.sin(spin)
    high, low = two_parts(np.block([[c, -s], [s, c]]))
    return across, back, twiddle, high, low


def split(value):
    high = value.astype(BF)
    return high, (value - high.astype(F32)).astype(BF)


def dot(left, right):
    return jnp.dot(left, right, preferred_element_type=F32)


def placement():
    upper = lax.axis_index("ch") >= 2
    row = lax.broadcasted_iota(jnp.int32, (WIDTH, WIDTH), 0)
    column = lax.broadcasted_iota(jnp.int32, (WIDTH, WIDTH), 1)
    group = row % ACROSS
    group = jnp.where(upper, ACROSS - 1 - group, group)
    return jnp.where(column == row - row % ACROSS + group, 1.0, 0.0).astype(BF)


def pack_kernel(count, *refs):
    ins, out = refs[:-1], refs[-1]
    place = placement()
    rows = count * 8
    index = 0
    for ref in ins:
        for b in range(ref.shape[0]):
            value = ref[b]
            turned = jnp.zeros((WIDTH, WIDTH), F32)
            for part in split(value):
                turned = turned + lax.dot_general(
                    place, part, (((1,), (1,)), ((), ())), preferred_element_type=F32
                )
            for q in range(4):
                for half in range(2):
                    row = (index * 4 + q) * 2 + half
                    out[pl.ds(row, ACROSS, stride=rows), :] = turned[
                        q * ACROSS : (q + 1) * ACROSS, half * 128 : (half + 1) * 128
                    ]
            index += 1


def unpack_kernel(ref, out):
    place = placement()
    count = out.shape[0]
    rows = count * 8
    for b in range(count):
        pieces = []
        for q in range(4):
            halves = [
                ref[pl.ds((b * 4 + q) * 2 + half, ACROSS, stride=rows), :] for half in range(2)
            ]
            pieces.append(jnp.concatenate(halves, 1))
        value = jnp.concatenate(pieces, 0).T
        total = jnp.zeros((WIDTH, WIDTH), F32)
        for part in split(value):
            total = total + dot(part, place)
        out[b] = total


def load_pair(ref, rows, first):
    pieces = [ref[pl.ds(first * 2 + k, ACROSS, stride=rows), :] for k in range(4)]
    return jnp.concatenate(pieces, 1)


def spectra_of(load, count, across, twiddle, high_ref, low_ref, stage_hi, stage_lo, out, first):
    cos, sin = twiddle[0], twiddle[1]
    for pair in range(count // 2):
        high, low = split(load(pair * 2))
        part = dot(across[...], jnp.concatenate([high, high, low], 0))
        turned = []
        for k in range(2):
            re = part[:HALF, k * WIDTH : (k + 1) * WIDTH]
            im = part[HALF:, k * WIDTH : (k + 1) * WIDTH]
            turned.append(jnp.concatenate([re * cos + im * sin, im * cos - re * sin], 1))
        high, low = split(jnp.concatenate(turned, 0))
        stage_hi[pair * 80 : pair * 80 + 80] = high
        stage_lo[pair * 80 : pair * 80 + 80] = low
    size = count * HALF
    high, low = stage_hi[:size], stage_lo[:size]
    whole = dot(high, high_ref[...]) + (dot(low, high_ref[...]) + dot(high, low_ref[...]))
    out[first * HALF : first * HALF + size] = whole


def positions_of(spectra, count, back, twiddle, high_ref, low_ref, store):
    high, low = split(spectra)
    whole = dot(high, high_ref[...]) + (dot(low, high_ref[...]) + dot(high, low_ref[...]))
    cos, sin = twiddle[0], twiddle[1]
    for pair in range(count // 2):
        sides = []
        for k in range(2):
            piece = whole[(pair * 2 + k) * HALF : (pair * 2 + k + 1) * HALF]
            re, im = piece[:, :WIDTH], piece[:, WIDTH:]
            sides.append(jnp.concatenate([re * cos + im * sin, im * cos - re * sin], 0))
        high, low = split(jnp.concatenate(sides, 1))
        store(pair * 2, dot(back[...], jnp.concatenate([high, high, low], 0)))


def store_pair(ref, rows, first, value):
    for k in range(4):
        ref[pl.ds(first * 2 + k, ACROSS, stride=rows), :] = value[:, k * 128 : (k + 1) * 128]


def grads_kernel(got, mirrored, across, back, twiddle, high, low, out, kept, spec, stage_hi, stage_lo):
    spectra_of(lambda n: load_pair(got, 40, n), 20, across, twiddle, high, low, stage_hi, stage_lo, spec, 0)
    spectra_of(lambda n: load_pair(mirrored, 8, n), 4, across, twiddle, high, low, stage_hi, stage_lo, spec, 20)
    kept[...] = spec[: 16 * HALF]
    products = []
    for n in range(16):
        q = n % 4
        own = spec[(16 + q) * HALF : (17 + q) * HALF]
        other = spec[(20 + 3 - q) * HALF : (24 - q) * HALF]
        er = own[:, :WIDTH] + other[:, :WIDTH]
        ei = own[:, WIDTH:] - other[:, WIDTH:]
        cot = spec[n * HALF : (n + 1) * HALF]
        cr, ci = cot[:, :WIDTH], cot[:, WIDTH:]
        products.append(jnp.concatenate([er * cr + ei * ci, ei * cr - er * ci], 1))
    positions_of(
        jnp.concatenate(products, 0), 16, back, twiddle, high, low, functools.partial(store_pair, out, 32)
    )


def cross_kernel(got, kept, across, twiddle, high, low, out, spec, stage_hi, stage_lo):
    spectra_of(lambda n: load_pair(got, 32, n), 16, across, twiddle, high, low, stage_hi, stage_lo, spec, 0)
    for q in range(4):
        re = jnp.zeros((HALF, WIDTH), F32)
        im = jnp.zeros((HALF, WIDTH), F32)
        for b in range(4):
            n = b * 4 + q
            x, c = spec[n * HALF : (n + 1) * HALF], kept[n * HALF : (n + 1) * HALF]
            xr, xi, cr, ci = x[:, :WIDTH], x[:, WIDTH:], c[:, :WIDTH], c[:, WIDTH:]
            re = re + (cr * xr + ci * xi)
            im = im + (cr * xi - ci * xr)
        out[q * HALF : (q + 1) * HALF] = jnp.concatenate([re, im], 1)


def filter_kernel(own, other, back, twiddle, high, low, out):
    rows = []
    for q in range(4):
        a = own[q * HALF : (q + 1) * HALF]
        b = other[(3 - q) * HALF : (4 - q) * HALF]
        rows.append(jnp.concatenate([a[:, :WIDTH] + b[:, :WIDTH], a[:, WIDTH:] - b[:, WIDTH:]], 1))
    positions_of(
        jnp.concatenate(rows, 0), 4, back, twiddle, high, low, functools.partial(store_pair, out, 8)
    )


def call(kernel, shapes, scratch, flops, *args):
    moved = sum(a.size * a.dtype.itemsize for a in args) + sum(4 * math.prod(s) for s in shapes)
    out = pl.pallas_call(
        kernel,
        out_shape=[jax.ShapeDtypeStruct(s, F32) for s in shapes],
        scratch_shapes=scratch,
        compiler_params=pltpu.CompilerParams(vmem_limit_bytes=VMEM),
        cost_estimate=pl.CostEstimate(flops=flops, bytes_accessed=moved, transcendentals=0),
    )(*args)
    return out[0] if len(shapes) == 1 else out


def swap(value):
    return lax.ppermute(value, "ch", [(s, 3 - s) for s in range(4)])


def exchange(value):
    blocks = value.reshape(ACROSS, -1, 128)
    return lax.all_to_all(blocks, "ctx", 0, 0, tiled=True).reshape(-1, 128)


def body(inputs, cotangent, filters):
    across, back, twiddle, high, low = [jnp.asarray(t) for t in tables()]
    filters = filters[None]
    stages = [pltpu.VMEM((20 * HALF, 2 * WIDTH), BF)] * 2
    first = call(functools.partial(pack_kernel, 5), [(ACROSS * 40, 128)], [], 10**9, cotangent, filters)
    second = call(functools.partial(pack_kernel, 4), [(ACROSS * 32, 128)], [], 10**9, inputs)
    first = exchange(first)
    second = exchange(second)
    mirrored = swap(first.reshape(ACROSS, 40, 128)[:, 32:].reshape(ACROSS * 8, 128))
    grads, kept = call(
        grads_kernel,
        [(ACROSS * 32, 128), (16 * HALF, 2 * WIDTH)],
        [pltpu.VMEM((24 * HALF, 2 * WIDTH), F32)] + stages,
        5 * 10**9,
        first, mirrored, across, back, twiddle, high, low,
    )
    cross = call(
        cross_kernel,
        [(4 * HALF, 2 * WIDTH)],
        [pltpu.VMEM((16 * HALF, 2 * WIDTH), F32)] + stages,
        2 * 10**9,
        second, kept, across, twiddle, high, low,
    )
    filter_grad = call(
        filter_kernel, [(ACROSS * 8, 128)], [], 10**9, cross, swap(cross), back, twiddle, high, low
    )
    input_grad = call(unpack_kernel, [(4, WIDTH, WIDTH)], [], 10**9, exchange(grads))
    filter_grad = call(unpack_kernel, [(1, WIDTH, WIDTH)], [], 10**9, exchange(filter_grad))
    return (input_grad, filter_grad[0])


def solution(mesh):
    in_specs = (P(None, "ctx", "ch"), P(None, "ctx", "ch"), P("ctx", "ch"))
    out_specs = (P(None, "ctx", "ch"), P("ctx", "ch"))
    return jax.shard_map(body, mesh=mesh, in_specs=in_specs, out_specs=out_specs, check_vma=False)
```

```python
import functools
import math

import jax
import jax.numpy as jnp
import numpy as np
from jax import lax
from jax.experimental import pallas as pl
from jax.experimental.pallas import tpu as pltpu
from jax.sharding import PartitionSpec as P

BF = jnp.bfloat16
F32 = jnp.float32
ACROSS = 64
DEVICES = 256
WIDTH = 256
PERIOD = ACROSS * WIDTH
HALF = 40
KEEP = ACROSS // 2 + 1
FACTOR = 1.0 / (PERIOD * math.sqrt(2.0 * PERIOD))
VMEM = 48 * 1024 * 1024


def two_parts(table):
    high = np.asarray(table, np.float32).astype(jnp.bfloat16)
    low = (table - high.astype(np.float64)).astype(np.float32).astype(jnp.bfloat16)
    return high, low


def tables():
    p = np.arange(HALF)
    i = np.arange(ACROSS)
    keep = (p < KEEP).astype(np.float64)
    angle = 2.0 * np.pi * (np.outer(p, i) % ACROSS) / ACROSS
    cos, sin = np.cos(angle) * keep[:, None], np.sin(angle) * keep[:, None]
    high, low = two_parts(np.concatenate([cos, -sin], 0))
    across = np.concatenate([high, low, high], 1)
    weight = np.where((p == 0) | (p == KEEP - 1), 1.0, 2.0) * keep * FACTOR
    back = np.concatenate([cos * weight[:, None], sin * weight[:, None]], 0).T
    high, low = two_parts(back)
    back = np.concatenate([high, low, high], 1)
    j = np.arange(WIDTH)
    turn = 2.0 * np.pi * np.outer(p, j) / PERIOD
    twiddle = np.stack([np.cos(turn), np.sin(turn)]).astype(np.float32)
    spin = 2.0 * np.pi * (np.outer(j, j) % WIDTH) / WIDTH
    c, s = np.cos(spin), np.sin(spin)
    high, low = two_parts(np.block([[c, -s], [s, c]]))
    return across, back, twiddle, high, low


def split(value):
    high = value.astype(BF)
    return high, (value - high.astype(F32)).astype(BF)


def dot(left, right):
    return jnp.dot(left, right, preferred_element_type=F32)


def placement():
    upper = lax.axis_index("ch") >= 2
    row = lax.broadcasted_iota(jnp.int32, (WIDTH, WIDTH), 0)
    column = lax.broadcasted_iota(jnp.int32, (WIDTH, WIDTH), 1)
    return jnp.where(column == jnp.where(upper, WIDTH - 1 - row, row), 1.0, 0.0).astype(BF)


def pack_kernel(cotangent, filters, inputs, out, held, sems):
    blocks = [cotangent.at[b] for b in range(4)] + [filters] + [inputs.at[b] for b in range(4)]
    copies = [pltpu.make_async_copy(block, held.at[u], sems.at[u]) for u, block in enumerate(blocks)]
    for copy in copies:
        copy.start()
    place = placement()
    for u, copy in enumerate(copies):
        copy.wait()
        turned = jnp.zeros((WIDTH, WIDTH), F32)
        for part in split(held[u]):
            turned = turned + lax.dot_general(
                place, part, (((1,), (1,)), ((), ())), preferred_element_type=F32
            )
        for half in range(2):
            out[pl.ds(u * 2 + half, DEVICES, stride=18), :] = turned[:, half * 128 : (half + 1) * 128]


def unpack_kernel(ref, inputs, filters, held, sems):
    place = placement()
    blocks = [inputs.at[b] for b in range(4)] + [filters]
    copies = []
    for u, block in enumerate(blocks):
        halves = [ref[pl.ds(u * 2 + half, DEVICES, stride=10), :] for half in range(2)]
        value = jnp.concatenate(halves, 1).T
        total = jnp.zeros((WIDTH, WIDTH), F32)
        for part in split(value):
            total = total + dot(part, place)
        held[u] = total
        copies.append(pltpu.make_async_copy(held.at[u], block, sems.at[u]))
        copies[-1].start()
    for copy in copies:
        copy.wait()


def load_pair(ref, first):
    pieces = []
    for n in (first, first + 1):
        for half in range(2):
            row = ((n % 4) * 9 + n // 4) * 2 + half
            pieces.append(ref[pl.ds(row, ACROSS, stride=72), :])
    return jnp.concatenate(pieces, 1)


def spectra_of(load, count, across, twiddle, high_ref, low_ref, stage_hi, stage_lo, out, first):
    cos, sin = twiddle[0], twiddle[1]
    for pair in range(count // 2):
        high, low = split(load(pair * 2))
        part = dot(across[...], jnp.concatenate([high, high, low], 0))
        turned = []
        for k in range(2):
            re = part[:HALF, k * WIDTH : (k + 1) * WIDTH]
            im = part[HALF:, k * WIDTH : (k + 1) * WIDTH]
            turned.append(jnp.concatenate([re * cos + im * sin, im * cos - re * sin], 1))
        high, low = split(jnp.concatenate(turned, 0))
        stage_hi[pair * 80 : pair * 80 + 80] = high
        stage_lo[pair * 80 : pair * 80 + 80] = low
    size = count * HALF
    high, low = stage_hi[:size], stage_lo[:size]
    whole = dot(high, high_ref[...]) + (dot(low, high_ref[...]) + dot(high, low_ref[...]))
    out[first * HALF : first * HALF + size] = whole


def positions_of(spectra, count, back, twiddle, high_ref, low_ref, store):
    high, low = split(spectra)
    whole = dot(high, high_ref[...]) + (dot(low, high_ref[...]) + dot(high, low_ref[...]))
    cos, sin = twiddle[0], twiddle[1]
    for pair in range(count // 2):
        sides = []
        for k in range(2):
            piece = whole[(pair * 2 + k) * HALF : (pair * 2 + k + 1) * HALF]
            re, im = piece[:, :WIDTH], piece[:, WIDTH:]
            sides.append(jnp.concatenate([re * cos + im * sin, im * cos - re * sin], 0))
        high, low = split(jnp.concatenate(sides, 1))
        store(pair * 2, dot(back[...], jnp.concatenate([high, high, low], 0)))


def store_pair(ref, first, value):
    for k in range(4):
        n = first + k // 2
        row = ((n % 4) * 5 + n // 4) * 2 + k % 2
        ref[pl.ds(row, ACROSS, stride=40), :] = value[:, k * 128 : (k + 1) * 128]


def grads_kernel(got, across, back, twiddle, high, low, out, spec, stage_hi, stage_lo):
    load = functools.partial(load_pair, got)
    spectra_of(load, 36, across, twiddle, high, low, stage_hi, stage_lo, spec, 0)
    products = []
    for n in range(16):
        s = n % 4
        own = spec[(16 + s) * HALF : (17 + s) * HALF]
        other = spec[(19 - s) * HALF : (20 - s) * HALF]
        er = own[:, :WIDTH] + other[:, :WIDTH]
        ei = own[:, WIDTH:] - other[:, WIDTH:]
        cot = spec[n * HALF : (n + 1) * HALF]
        cr, ci = cot[:, :WIDTH], cot[:, WIDTH:]
        products.append(jnp.concatenate([er * cr + ei * ci, ei * cr - er * ci], 1))
    crosses = []
    for s in range(4):
        re = jnp.zeros((HALF, WIDTH), F32)
        im = jnp.zeros((HALF, WIDTH), F32)
        for b in range(4):
            n = b * 4 + s
            c, x = spec[n * HALF : (n + 1) * HALF], spec[(20 + n) * HALF : (21 + n) * HALF]
            xr, xi, cr, ci = x[:, :WIDTH], x[:, WIDTH:], c[:, :WIDTH], c[:, WIDTH:]
            re = re + (cr * xr + ci * xi)
            im = im + (cr * xi - ci * xr)
        crosses.append((re, im))
    for s in range(4):
        a, b = crosses[s], crosses[3 - s]
        products.append(jnp.concatenate([a[0] + b[0], a[1] - b[1]], 1))
    positions_of(
        jnp.concatenate(products, 0), 20, back, twiddle, high, low, functools.partial(store_pair, out)
    )


def call(kernel, outs, scratch, flops, *args, in_specs=None, out_specs=None):
    moved = sum(a.size * a.dtype.itemsize for a in args) + sum(4 * math.prod(o) for o in outs)
    options = dict(in_specs=in_specs) if in_specs else {}
    if out_specs:
        options["out_specs"] = out_specs
    return pl.pallas_call(
        kernel,
        out_shape=[jax.ShapeDtypeStruct(o, F32) for o in outs],
        scratch_shapes=scratch,
        compiler_params=pltpu.CompilerParams(vmem_limit_bytes=VMEM),
        cost_estimate=pl.CostEstimate(flops=flops, bytes_accessed=moved, transcendentals=0),
        **options,
    )(*args)


def exchange(value, units):
    blocks = value.reshape(DEVICES, units, 2, 128)
    return lax.all_to_all(blocks, ("ctx", "ch"), 0, 0, tiled=True).reshape(-1, 128)


def body(inputs, cotangent, filters):
    across, back, twiddle, high, low = [jnp.asarray(t) for t in tables()]
    anywhere = pl.BlockSpec(memory_space=pl.ANY)
    (packed,) = call(
        pack_kernel,
        [(DEVICES * 18, 128)],
        [pltpu.VMEM((9, WIDTH, WIDTH), F32), pltpu.SemaphoreType.DMA((9,))],
        10**9,
        cotangent, filters, inputs,
        in_specs=[anywhere] * 3,
    )
    got = exchange(packed, 9)
    (grads,) = call(
        grads_kernel,
        [(DEVICES * 10, 128)],
        [pltpu.VMEM((36 * HALF, 2 * WIDTH), F32)] + [pltpu.VMEM((36 * HALF, 2 * WIDTH), BF)] * 2,
        8 * 10**9,
        got, across, back, twiddle, high, low,
    )
    return tuple(
        call(
            unpack_kernel,
            [(4, WIDTH, WIDTH), (WIDTH, WIDTH)],
            [pltpu.VMEM((5, WIDTH, WIDTH), F32), pltpu.SemaphoreType.DMA((5,))],
            10**9,
            exchange(grads, 5),
            out_specs=[anywhere] * 2,
        )
    )


def solution(mesh):
    in_specs = (P(None, "ctx", "ch"), P(None, "ctx", "ch"), P("ctx", "ch"))
    out_specs = (P(None, "ctx", "ch"), P("ctx", "ch"))
    return jax.shard_map(body, mesh=mesh, in_specs=in_specs, out_specs=out_specs, check_vma=False)
```

```python
import functools
import math

import jax
import jax.numpy as jnp
import numpy as np
from jax import lax
from jax.experimental import pallas as pl
from jax.experimental.pallas import tpu as pltpu
from jax.sharding import PartitionSpec as P

BF = jnp.bfloat16
F32 = jnp.float32
ACROSS = 64
DEVICES = 256
WIDTH = 256
PERIOD = ACROSS * WIDTH
HALF = ACROSS // 2
FACTOR = 1.0 / (PERIOD * math.sqrt(2.0 * PERIOD))
VMEM = 48 * 1024 * 1024
PACK_VMEM = 56 * 1024 * 1024


def two_parts(table):
    high = np.asarray(table, np.float32).astype(jnp.bfloat16)
    low = (table - high.astype(np.float64)).astype(np.float32).astype(jnp.bfloat16)
    return high, low


def tables():
    p = np.arange(HALF)
    i = np.arange(ACROSS)
    angle = 2.0 * np.pi * (np.outer(p, i) % ACROSS) / ACROSS
    cos, sin = np.cos(angle), np.sin(angle)
    last = np.cos(np.pi * i)
    fore = np.concatenate([cos, -sin], 0)
    fore[HALF] = last
    high, low = two_parts(fore)
    across = np.concatenate([high, low, high], 1)
    weight = np.where(p == 0, 1.0, 2.0)[:, None] * FACTOR
    back = np.concatenate([cos * weight, sin * weight], 0)
    back[HALF] = last * FACTOR
    high, low = two_parts(back.T)
    back = np.concatenate([high, low, high], 1)
    j = np.arange(WIDTH)
    turn = 2.0 * np.pi * np.outer(np.arange(HALF + 1), j) / PERIOD
    c, s = np.cos(turn), np.sin(turn)
    masked = c[:HALF] * (p > 0)[:, None]
    ends = np.zeros((HALF, WIDTH))
    ends[0], ends[1] = c[HALF], s[HALF]
    twiddle = np.stack([c[:HALF], s[:HALF], masked, ends]).astype(np.float32)
    spin = 2.0 * np.pi * (np.outer(j, j) % WIDTH) / WIDTH
    c, s = np.cos(spin), np.sin(spin)
    high, low = two_parts(np.block([[c, -s], [s, c]]))
    return across, back, twiddle, np.concatenate([high, high, low], 0)


def split(value):
    high = value.astype(BF)
    return high, (value - high.astype(F32)).astype(BF)


def dot(left, right):
    return jnp.dot(left, right, preferred_element_type=F32)


def placement():
    upper = lax.axis_index("ch") >= 2
    row = lax.broadcasted_iota(jnp.int32, (WIDTH, WIDTH), 0)
    column = lax.broadcasted_iota(jnp.int32, (WIDTH, WIDTH), 1)
    return jnp.where(column == jnp.where(upper, WIDTH - 1 - row, row), 1.0, 0.0).astype(BF)


def pack_kernel(cotangent, filters, inputs, out, held, sems):
    blocks = [cotangent.at[b] for b in range(4)] + [filters] + [inputs.at[b] for b in range(4)]
    copies = [pltpu.make_async_copy(block, held.at[u], sems.at[u]) for u, block in enumerate(blocks)]
    for copy in copies:
        copy.start()
    place = placement()
    for u, copy in enumerate(copies):
        copy.wait()
        high, low = split(held[u])
        turned = (dot(high, place) + dot(low, place)).T
        for half in range(2):
            out[pl.ds(u * 2 + half, DEVICES, stride=18), :] = turned[:, half * 128 : (half + 1) * 128]


def unpack_kernel(ref, inputs, filters, held, sems):
    place = placement()
    blocks = [inputs.at[b] for b in range(4)] + [filters]
    copies = []
    for u, block in enumerate(blocks):
        halves = [ref[pl.ds(u * 2 + half, DEVICES, stride=10), :] for half in range(2)]
        value = jnp.concatenate(halves, 1).T
        total = jnp.zeros((WIDTH, WIDTH), F32)
        for part in split(value):
            total = total + dot(part, place)
        held[u] = total
        copies.append(pltpu.make_async_copy(held.at[u], block, sems.at[u]))
        copies[-1].start()
    for copy in copies:
        copy.wait()


def load_pair(ref, first):
    pieces = []
    for n in (first, first + 1):
        for half in range(2):
            row = ((n % 4) * 9 + n // 4) * 2 + half
            pieces.append(ref[pl.ds(row, ACROSS, stride=72), :])
    return jnp.concatenate(pieces, 1)


def spin_rows(high, low, table):
    return dot(jnp.concatenate([high, low, high], 1), table[...])


def spectra_of(load, count, across, twiddle, table, stage_hi, stage_lo, ends, spec):
    cos, sin, masked = twiddle[0], twiddle[1], twiddle[2]
    for pair in range(count // 2):
        high, low = split(load(pair * 2))
        part = dot(across[...], jnp.concatenate([high, high, low], 0))
        turned = []
        for k in range(2):
            re = part[:HALF, k * WIDTH : (k + 1) * WIDTH]
            im = part[HALF:, k * WIDTH : (k + 1) * WIDTH]
            ends[pair * 2 + k : pair * 2 + k + 1, :] = im[:1]
            turned.append(jnp.concatenate([re * cos + im * sin, im * masked - re * sin], 1))
        high, low = split(jnp.concatenate(turned, 0))
        stage_hi[pair * 64 : pair * 64 + 64] = high
        stage_lo[pair * 64 : pair * 64 + 64] = low
    base, more = count * HALF, ends.shape[0]
    last = ends[...]
    high, low = split(jnp.concatenate([last * twiddle[3, 0:1], -last * twiddle[3, 1:2]], 1))
    stage_hi[base : base + more] = high
    stage_lo[base : base + more] = low
    spec[...] = spin_rows(stage_hi[: base + more], stage_lo[: base + more], table)


def positions_of(count, back, twiddle, table, stage_hi, stage_lo, spec, store):
    base = count * HALF
    size = base + 32
    spec[:size] = spin_rows(stage_hi[:size], stage_lo[:size], table)
    cos, sin = twiddle[0], twiddle[1]
    first = lax.broadcasted_iota(jnp.int32, (8, WIDTH), 0) == 0
    ends = spec[base:size]
    ends = ends[:, :WIDTH] * twiddle[3, 0:1] + ends[:, WIDTH:] * twiddle[3, 1:2]
    for pair in range(count // 2):
        sides = []
        for k in range(2):
            n = pair * 2 + k
            piece = spec[n * HALF : (n + 1) * HALF]
            re, im = piece[:, :WIDTH], piece[:, WIDTH:]
            im, re = im * cos - re * sin, re * cos + im * sin
            top = jnp.where(first, jnp.broadcast_to(ends[n : n + 1], (8, WIDTH)), im[:8])
            sides.append(jnp.concatenate([re, top, im[8:]], 0))
        high, low = split(jnp.concatenate(sides, 1))
        store(pair * 2, dot(back[...], jnp.concatenate([high, high, low], 0)))


def store_pair(ref, first, value):
    for k in range(4):
        n = first + k // 2
        row = ((n % 4) * 5 + n // 4) * 2 + k % 2
        ref[pl.ds(row, ACROSS, stride=40), :] = value[:, k * 128 : (k + 1) * 128]


def grads_kernel(got, across, back, twiddle, table, out, spec, stage_hi, stage_lo, ends, extra):
    load = functools.partial(load_pair, got)
    spectra_of(load, 36, across, twiddle, table, stage_hi, stage_lo, ends, spec)
    for tail in (False, True):

        def take(n):
            rows = spec[36 * HALF + n : 36 * HALF + n + 1] if tail else spec[n * HALF : (n + 1) * HALF]
            return rows[:, :WIDTH], rows[:, WIDTH:]

        def put(n, re, im):
            rows = jnp.concatenate([re, im], 1)
            if tail:
                extra[n : n + 1] = rows
            else:
                high, low = split(rows)
                stage_hi[n * HALF : (n + 1) * HALF] = high
                stage_lo[n * HALF : (n + 1) * HALF] = low

        crosses = []
        for s in range(4):
            own, other = take(16 + s), take(19 - s)
            er, ei = own[0] + other[0], own[1] - other[1]
            re = im = 0.0
            for b in range(4):
                n = b * 4 + s
                (cr, ci), (xr, xi) = take(n), take(20 + n)
                put(n, er * cr + ei * ci, ei * cr - er * ci)
                re = re + (cr * xr + ci * xi)
                im = im + (cr * xi - ci * xr)
            crosses.append((re, im))
        for s in range(4):
            a, b = crosses[s], crosses[3 - s]
            put(16 + s, a[0] + b[0], a[1] - b[1])
    high, low = split(extra[...])
    stage_hi[20 * HALF : 20 * HALF + 32] = high
    stage_lo[20 * HALF : 20 * HALF + 32] = low
    positions_of(
        20, back, twiddle, table, stage_hi, stage_lo, spec, functools.partial(store_pair, out)
    )


def call(kernel, outs, scratch, flops, *args, in_specs=None, out_specs=None, vmem=VMEM, near=False):
    moved = sum(a.size * a.dtype.itemsize for a in args) + sum(4 * math.prod(o) for o in outs)
    options = dict(in_specs=in_specs) if in_specs else {}
    if out_specs:
        options["out_specs"] = out_specs
    return pl.pallas_call(
        kernel,
        out_shape=[(pltpu.VMEM if near else jax.ShapeDtypeStruct)(o, F32) for o in outs],
        scratch_shapes=scratch,
        compiler_params=pltpu.CompilerParams(vmem_limit_bytes=vmem),
        cost_estimate=pl.CostEstimate(flops=flops, bytes_accessed=moved, transcendentals=0),
        **options,
    )(*args)


def exchange(value, units):
    blocks = value.reshape(DEVICES, units, 2, 128)
    return lax.all_to_all(blocks, ("ctx", "ch"), 0, 0, tiled=True).reshape(-1, 128)


def body(inputs, cotangent, filters):
    across, back, twiddle, table = [jnp.asarray(t) for t in tables()]
    far = pl.BlockSpec(memory_space=pltpu.HBM)
    (packed,) = call(
        pack_kernel,
        [(DEVICES * 18, 128)],
        [pltpu.VMEM((9, WIDTH, WIDTH), F32), pltpu.SemaphoreType.DMA((9,))],
        10**9,
        cotangent, filters, inputs,
        in_specs=[far] * 3,
        vmem=PACK_VMEM,
        near=True,
    )
    got = exchange(packed, 9)
    (grads,) = call(
        grads_kernel,
        [(DEVICES * 10, 128)],
        [pltpu.VMEM((36 * HALF + 48, 2 * WIDTH), F32)]
        + [pltpu.VMEM((36 * HALF + 48, 2 * WIDTH), BF)] * 2
        + [pltpu.VMEM((48, WIDTH), F32), pltpu.VMEM((32, 2 * WIDTH), F32)],
        8 * 10**9,
        got, across, back, twiddle, table,
    )
    return tuple(
        call(
            unpack_kernel,
            [(4, WIDTH, WIDTH), (WIDTH, WIDTH)],
            [pltpu.VMEM((5, WIDTH, WIDTH), F32), pltpu.SemaphoreType.DMA((5,))],
            10**9,
            exchange(grads, 5),
            out_specs=[far] * 2,
        )
    )


def solution(mesh):
    in_specs = (P(None, "ctx", "ch"), P(None, "ctx", "ch"), P("ctx", "ch"))
    out_specs = (P(None, "ctx", "ch"), P("ctx", "ch"))
    return jax.shard_map(body, mesh=mesh, in_specs=in_specs, out_specs=out_specs, check_vma=False)
```

```python
import functools
import math

import jax
import jax.numpy as jnp
import numpy as np
from jax import lax
from jax.experimental import pallas as pl
from jax.experimental.pallas import tpu as pltpu
from jax.sharding import PartitionSpec as P

BF = jnp.bfloat16
F32 = jnp.float32
ACROSS = 64
DEVICES = 256
WIDTH = 256
PART = WIDTH // 2
PERIOD = ACROSS * WIDTH
HALF = ACROSS // 2
FACTOR = 1.0 / (PERIOD * math.sqrt(2.0 * PERIOD))
VMEM = 48 * 1024 * 1024
PACK_VMEM = 56 * 1024 * 1024


def two_parts(table):
    high = np.asarray(table, np.float32).astype(jnp.bfloat16)
    low = (table - high.astype(np.float64)).astype(np.float32).astype(jnp.bfloat16)
    return high, low


def tables():
    p = np.arange(HALF)
    i = np.arange(ACROSS)
    angle = 2.0 * np.pi * (np.outer(p, i) % ACROSS) / ACROSS
    cos, sin = np.cos(angle), np.sin(angle)
    last = np.cos(np.pi * i)
    fore = np.concatenate([cos, -sin], 0)
    fore[HALF] = last
    high, low = two_parts(fore)
    across = np.concatenate([high, low, high], 1)
    weight = np.where(p == 0, 1.0, 2.0)[:, None] * FACTOR
    back = np.concatenate([cos * weight, sin * weight], 0)
    back[HALF] = last * FACTOR
    high, low = two_parts(back.T)
    back = np.concatenate([high, low, high], 1)
    j = np.arange(WIDTH)
    turn = 2.0 * np.pi * np.outer(np.arange(HALF + 1), j) / PERIOD
    c, s = np.cos(turn), np.sin(turn)
    masked = c[:HALF] * (p > 0)[:, None]
    ends = np.zeros((HALF, WIDTH))
    ends[0], ends[1] = c[HALF], s[HALF]
    twiddle = np.stack([c[:HALF], s[:HALF], masked, ends]).astype(np.float32)
    j = np.arange(PART)
    parts = []
    for turns in (2 * np.outer(j, j), np.outer(j, 2 * j + 1), np.outer(2 * j + 1, j)):
        spin = 2.0 * np.pi * (turns % WIDTH) / WIDTH
        c, s = np.cos(spin), np.sin(spin)
        high, low = two_parts(np.block([[c, -s], [s, c]]))
        parts.append(np.concatenate([high, high, low], 0))
    return across, back, twiddle, np.stack(parts)


def split(value):
    high = value.astype(BF)
    return high, (value - high.astype(F32)).astype(BF)


def dot(left, right):
    return jnp.dot(left, right, preferred_element_type=F32)


def placement():
    upper = lax.axis_index("ch") >= 2
    row = lax.broadcasted_iota(jnp.int32, (WIDTH, WIDTH), 0)
    column = lax.broadcasted_iota(jnp.int32, (WIDTH, WIDTH), 1)
    return jnp.where(column == jnp.where(upper, WIDTH - 1 - row, row), 1.0, 0.0).astype(BF)


def pack_kernel(cotangent, filters, inputs, out, held, sems):
    blocks = [cotangent.at[b] for b in range(4)] + [filters] + [inputs.at[b] for b in range(4)]
    copies = [pltpu.make_async_copy(block, held.at[u], sems.at[u]) for u, block in enumerate(blocks)]
    for copy in copies[:3]:
        copy.start()
    place = placement()
    for u, copy in enumerate(copies):
        copy.wait()
        if u + 3 < len(copies):
            copies[u + 3].start()
        high, low = split(held[u])
        turned = (dot(high, place) + dot(low, place)).T
        for half in range(2):
            out[pl.ds(u * 2 + half, DEVICES, stride=18), :] = turned[:, half * 128 : (half + 1) * 128]


def unpack_kernel(ref, inputs, filters, held, sems):
    place = placement()
    blocks = [inputs.at[b] for b in range(4)] + [filters]
    copies = []
    for u, block in enumerate(blocks):
        halves = [ref[pl.ds(u * 2 + half, DEVICES, stride=10), :] for half in range(2)]
        value = jnp.concatenate(halves, 1).T
        total = jnp.zeros((WIDTH, WIDTH), F32)
        for part in split(value):
            total = total + dot(part, place)
        held[u] = total
        copies.append(pltpu.make_async_copy(held.at[u], block, sems.at[u]))
        copies[-1].start()
    for copy in copies:
        copy.wait()


def load_pair(ref, first):
    pieces = []
    for n in (first, first + 1):
        for half in range(2):
            row = ((n % 4) * 9 + n // 4) * 2 + half
            pieces.append(ref[pl.ds(row, ACROSS, stride=72), :])
    return jnp.concatenate(pieces, 1)


def spin_rows(high, low, table, odd):
    results = []
    for k, which in enumerate((0, odd)):
        h = jnp.concatenate([high[:, k * PART : (k + 1) * PART], high[:, (k + 2) * PART : (k + 3) * PART]], 1)
        l = jnp.concatenate([low[:, k * PART : (k + 1) * PART], low[:, (k + 2) * PART : (k + 3) * PART]], 1)
        results.append(dot(jnp.concatenate([h, l, h], 1), table[which]))
    return results


def butterfly(value):
    a, b = value[:, :PART], value[:, PART:]
    return [a + b, a - b]


def spectra_of(load, count, across, twiddle, table, stage_hi, stage_lo, ends, spec):
    cos, sin, masked = twiddle[0], twiddle[1], twiddle[2]
    for pair in range(count // 2):
        high, low = split(load(pair * 2))
        part = dot(across[...], jnp.concatenate([high, high, low], 0))
        turned = []
        for k in range(2):
            re = part[:HALF, k * WIDTH : (k + 1) * WIDTH]
            im = part[HALF:, k * WIDTH : (k + 1) * WIDTH]
            ends[pair * 2 + k : pair * 2 + k + 1, :] = im[:1]
            re, im = re * cos + im * sin, im * masked - re * sin
            turned.append(jnp.concatenate(butterfly(re) + butterfly(im), 1))
        high, low = split(jnp.concatenate(turned, 0))
        stage_hi[pair * 64 : pair * 64 + 64] = high
        stage_lo[pair * 64 : pair * 64 + 64] = low
    base, more = count * HALF, ends.shape[0]
    last = ends[...]
    pieces = butterfly(last * twiddle[3, 0:1]) + butterfly(-last * twiddle[3, 1:2])
    high, low = split(jnp.concatenate(pieces, 1))
    stage_hi[base : base + more] = high
    stage_lo[base : base + more] = low
    even, odd = spin_rows(stage_hi[: base + more], stage_lo[: base + more], table, 1)
    spec[:, 0 * PART : 1 * PART] = even[:, :PART]
    spec[:, 1 * PART : 2 * PART] = odd[:, :PART]
    spec[:, 2 * PART : 3 * PART] = even[:, PART:]
    spec[:, 3 * PART : 4 * PART] = odd[:, PART:]


def positions_of(count, back, twiddle, table, stage_hi, stage_lo, spec, store):
    base = count * HALF
    size = base + 32
    even, odd = spin_rows(stage_hi[:size], stage_lo[:size], table, 2)
    spec[:size, 0 * PART : 1 * PART] = even[:, :PART] + odd[:, :PART]
    spec[:size, 1 * PART : 2 * PART] = even[:, :PART] - odd[:, :PART]
    spec[:size, 2 * PART : 3 * PART] = even[:, PART:] + odd[:, PART:]
    spec[:size, 3 * PART : 4 * PART] = even[:, PART:] - odd[:, PART:]
    cos, sin = twiddle[0], twiddle[1]
    first = lax.broadcasted_iota(jnp.int32, (8, WIDTH), 0) == 0
    ends = spec[base:size]
    ends = ends[:, :WIDTH] * twiddle[3, 0:1] + ends[:, WIDTH:] * twiddle[3, 1:2]
    for pair in range(count // 2):
        sides = []
        for k in range(2):
            n = pair * 2 + k
            piece = spec[n * HALF : (n + 1) * HALF]
            re, im = piece[:, :WIDTH], piece[:, WIDTH:]
            im, re = im * cos - re * sin, re * cos + im * sin
            top = jnp.where(first, jnp.broadcast_to(ends[n : n + 1], (8, WIDTH)), im[:8])
            sides.append(jnp.concatenate([re, top, im[8:]], 0))
        high, low = split(jnp.concatenate(sides, 1))
        store(pair * 2, dot(back[...], jnp.concatenate([high, high, low], 0)))


def store_pair(ref, first, value):
    for k in range(4):
        n = first + k // 2
        row = ((n % 4) * 5 + n // 4) * 2 + k % 2
        ref[pl.ds(row, ACROSS, stride=40), :] = value[:, k * 128 : (k + 1) * 128]


def grads_kernel(got, across, back, twiddle, table, out, spec, stage_hi, stage_lo, ends, extra):
    load = functools.partial(load_pair, got)
    spectra_of(load, 36, across, twiddle, table, stage_hi, stage_lo, ends, spec)
    for tail in (False, True):

        def take(n):
            rows = spec[36 * HALF + n : 36 * HALF + n + 1] if tail else spec[n * HALF : (n + 1) * HALF]
            return rows[:, :WIDTH], rows[:, WIDTH:]

        def put(n, re, im):
            rows = jnp.concatenate([re, im], 1)
            if tail:
                extra[n : n + 1] = rows
            else:
                high, low = split(rows)
                stage_hi[n * HALF : (n + 1) * HALF] = high
                stage_lo[n * HALF : (n + 1) * HALF] = low

        crosses = []
        for s in range(4):
            own, other = take(16 + s), take(19 - s)
            er, ei = own[0] + other[0], own[1] - other[1]
            re = im = 0.0
            for b in range(4):
                n = b * 4 + s
                (cr, ci), (xr, xi) = take(n), take(20 + n)
                put(n, er * cr + ei * ci, ei * cr - er * ci)
                re = re + (cr * xr + ci * xi)
                im = im + (cr * xi - ci * xr)
            crosses.append((re, im))
        for s in range(4):
            a, b = crosses[s], crosses[3 - s]
            put(16 + s, a[0] + b[0], a[1] - b[1])
    high, low = split(extra[...])
    stage_hi[20 * HALF : 20 * HALF + 32] = high
    stage_lo[20 * HALF : 20 * HALF + 32] = low
    positions_of(
        20, back, twiddle, table, stage_hi, stage_lo, spec, functools.partial(store_pair, out)
    )


def call(kernel, outs, scratch, flops, *args, in_specs=None, out_specs=None, vmem=VMEM, near=False):
    moved = sum(a.size * a.dtype.itemsize for a in args) + sum(4 * math.prod(o) for o in outs)
    options = dict(in_specs=in_specs) if in_specs else {}
    if out_specs:
        options["out_specs"] = out_specs
    return pl.pallas_call(
        kernel,
        out_shape=[(pltpu.VMEM if near else jax.ShapeDtypeStruct)(o, F32) for o in outs],
        scratch_shapes=scratch,
        compiler_params=pltpu.CompilerParams(vmem_limit_bytes=vmem),
        cost_estimate=pl.CostEstimate(flops=flops, bytes_accessed=moved, transcendentals=0),
        **options,
    )(*args)


def exchange(value, units):
    blocks = value.reshape(DEVICES, units, 2, 128)
    return lax.all_to_all(blocks, ("ctx", "ch"), 0, 0, tiled=True).reshape(-1, 128)


def body(inputs, cotangent, filters):
    across, back, twiddle, table = [jnp.asarray(t) for t in tables()]
    far = pl.BlockSpec(memory_space=pltpu.HBM)
    (packed,) = call(
        pack_kernel,
        [(DEVICES * 18, 128)],
        [pltpu.VMEM((9, WIDTH, WIDTH), F32), pltpu.SemaphoreType.DMA((9,))],
        10**9,
        cotangent, filters, inputs,
        in_specs=[far] * 3,
        vmem=PACK_VMEM,
        near=True,
    )
    got = exchange(packed, 9)
    (grads,) = call(
        grads_kernel,
        [(DEVICES * 10, 128)],
        [pltpu.VMEM((36 * HALF + 48, 2 * WIDTH), F32)]
        + [pltpu.VMEM((36 * HALF + 48, 2 * WIDTH), BF)] * 2
        + [pltpu.VMEM((48, WIDTH), F32), pltpu.VMEM((32, 2 * WIDTH), F32)],
        8 * 10**9,
        got, across, back, twiddle, table,
    )
    return tuple(
        call(
            unpack_kernel,
            [(4, WIDTH, WIDTH), (WIDTH, WIDTH)],
            [pltpu.VMEM((5, WIDTH, WIDTH), F32), pltpu.SemaphoreType.DMA((5,))],
            10**9,
            exchange(grads, 5),
            out_specs=[far] * 2,
        )
    )


def solution(mesh):
    in_specs = (P(None, "ctx", "ch"), P(None, "ctx", "ch"), P("ctx", "ch"))
    out_specs = (P(None, "ctx", "ch"), P("ctx", "ch"))
    return jax.shard_map(body, mesh=mesh, in_specs=in_specs, out_specs=out_specs, check_vma=False)
```

```python
import functools
import math

import jax
import jax.numpy as jnp
import numpy as np
from jax import lax
from jax.experimental import pallas as pl
from jax.experimental.pallas import tpu as pltpu
from jax.sharding import PartitionSpec as P

BF = jnp.bfloat16
F32 = jnp.float32
ACROSS = 64
DEVICES = 256
WIDTH = 256
PART = WIDTH // 2
PERIOD = ACROSS * WIDTH
HALF = ACROSS // 2
FACTOR = 1.0 / (PERIOD * math.sqrt(2.0 * PERIOD))
AHEAD = 7
VMEM = 48 * 1024 * 1024
PACK_VMEM = 56 * 1024 * 1024


def two_parts(table):
    high = np.asarray(table, np.float32).astype(jnp.bfloat16)
    low = (table - high.astype(np.float64)).astype(np.float32).astype(jnp.bfloat16)
    return high, low


def tables():
    p = np.arange(HALF)
    i = np.arange(ACROSS)
    angle = 2.0 * np.pi * (np.outer(p, i) % ACROSS) / ACROSS
    cos, sin = np.cos(angle), np.sin(angle)
    last = np.cos(np.pi * i)
    fore = np.concatenate([cos, -sin], 0)
    fore[HALF] = last
    high, low = two_parts(fore)
    across = np.concatenate([high, low, high], 1)
    weight = np.where(p == 0, 1.0, 2.0)[:, None] * FACTOR
    back = np.concatenate([cos * weight, sin * weight], 0)
    back[HALF] = last * FACTOR
    high, low = two_parts(back.T)
    back = np.concatenate([high, low, high], 1)
    j = np.arange(WIDTH)
    turn = 2.0 * np.pi * np.outer(np.arange(HALF + 1), j) / PERIOD
    c, s = np.cos(turn), np.sin(turn)
    masked = c[:HALF] * (p > 0)[:, None]
    ends = np.zeros((HALF, WIDTH))
    ends[0], ends[1] = c[HALF], s[HALF]
    twiddle = np.stack([c[:HALF], s[:HALF], masked, ends]).astype(np.float32)
    j = np.arange(PART)
    parts = []
    for turns in (2 * np.outer(j, j), np.outer(j, 2 * j + 1), np.outer(2 * j + 1, j)):
        spin = 2.0 * np.pi * (turns % WIDTH) / WIDTH
        c, s = np.cos(spin), np.sin(spin)
        high, low = two_parts(np.block([[c, -s], [s, c]]))
        parts.append(np.concatenate([high, high, low], 0))
    return across, back, twiddle, np.stack(parts)


def split(value):
    high = value.astype(BF)
    return high, (value - high.astype(F32)).astype(BF)


def dot(left, right):
    return jnp.dot(left, right, preferred_element_type=F32)


def mirrored(value):
    back = 7 - lax.broadcasted_iota(jnp.int32, (8, 128), 0)
    columns = []
    for half in range(2):
        lanes = slice(half * 128, (half + 1) * 128)
        groups = [value[k * 8 : (k + 1) * 8, lanes] for k in reversed(range(value.shape[0] // 8))]
        columns.append(
            jnp.concatenate([jnp.take_along_axis(group, back, axis=0) for group in groups], 0)
        )
    return jnp.concatenate(columns, 1)


def both_halves(run):
    upper = lax.axis_index("ch") >= 2
    pl.when(upper)(functools.partial(run, mirrored))
    pl.when(jnp.logical_not(upper))(functools.partial(run, lambda value: value))


def pack_kernel(cotangent, filters, inputs, out, held, sems):
    blocks = [cotangent.at[b] for b in range(4)] + [filters] + [inputs.at[b] for b in range(4)]
    copies = [pltpu.make_async_copy(block, held.at[u], sems.at[u]) for u, block in enumerate(blocks)]
    for copy in copies[:AHEAD]:
        copy.start()

    def run(order):
        for u, copy in enumerate(copies):
            copy.wait()
            if u + AHEAD < len(copies):
                copies[u + AHEAD].start()
            turned = order(held[u].T)
            for half in range(2):
                out[pl.ds(u * 2 + half, DEVICES, stride=18), :] = turned[
                    :, half * 128 : (half + 1) * 128
                ]

    both_halves(run)


def unpack_kernel(ref, inputs, filters, held, sems):
    blocks = [inputs.at[b] for b in range(4)] + [filters]
    copies = [pltpu.make_async_copy(held.at[u], block, sems.at[u]) for u, block in enumerate(blocks)]

    def run(order):
        for u, copy in enumerate(copies):
            halves = [ref[pl.ds(u * 2 + half, DEVICES, stride=10), :] for half in range(2)]
            held[u] = order(jnp.concatenate(halves, 1)).T
            copy.start()
        for copy in copies:
            copy.wait()

    both_halves(run)


def load_pair(ref, first):
    pieces = []
    for n in (first, first + 1):
        for half in range(2):
            row = ((n % 4) * 9 + n // 4) * 2 + half
            pieces.append(ref[pl.ds(row, ACROSS, stride=72), :])
    return jnp.concatenate(pieces, 1)


def spin_rows(high, low, table, odd):
    results = []
    for k, which in enumerate((0, odd)):
        h = jnp.concatenate([high[:, k * PART : (k + 1) * PART], high[:, (k + 2) * PART : (k + 3) * PART]], 1)
        l = jnp.concatenate([low[:, k * PART : (k + 1) * PART], low[:, (k + 2) * PART : (k + 3) * PART]], 1)
        results.append(dot(jnp.concatenate([h, l, h], 1), table[which]))
    return results


def butterfly(value):
    a, b = value[:, :PART], value[:, PART:]
    return [a + b, a - b]


def spectra_of(load, count, across, twiddle, table, stage_hi, stage_lo, ends, spec):
    cos, sin, masked = twiddle[0], twiddle[1], twiddle[2]
    for pair in range(count // 2):
        high, low = split(load(pair * 2))
        part = dot(across[...], jnp.concatenate([high, high, low], 0))
        turned = []
        for k in range(2):
            re = part[:HALF, k * WIDTH : (k + 1) * WIDTH]
            im = part[HALF:, k * WIDTH : (k + 1) * WIDTH]
            ends[pair * 2 + k : pair * 2 + k + 1, :] = im[:1]
            re, im = re * cos + im * sin, im * masked - re * sin
            turned.append(jnp.concatenate(butterfly(re) + butterfly(im), 1))
        high, low = split(jnp.concatenate(turned, 0))
        stage_hi[pair * 64 : pair * 64 + 64] = high
        stage_lo[pair * 64 : pair * 64 + 64] = low
    base, more = count * HALF, ends.shape[0]
    last = ends[...]
    pieces = butterfly(last * twiddle[3, 0:1]) + butterfly(-last * twiddle[3, 1:2])
    high, low = split(jnp.concatenate(pieces, 1))
    stage_hi[base : base + more] = high
    stage_lo[base : base + more] = low
    even, odd = spin_rows(stage_hi[: base + more], stage_lo[: base + more], table, 1)
    spec[:, 0 * PART : 1 * PART] = even[:, :PART]
    spec[:, 1 * PART : 2 * PART] = odd[:, :PART]
    spec[:, 2 * PART : 3 * PART] = even[:, PART:]
    spec[:, 3 * PART : 4 * PART] = odd[:, PART:]


def positions_of(count, back, twiddle, table, stage_hi, stage_lo, spec, store):
    base = count * HALF
    size = base + 32
    even, odd = spin_rows(stage_hi[:size], stage_lo[:size], table, 2)
    spec[:size, 0 * PART : 1 * PART] = even[:, :PART] + odd[:, :PART]
    spec[:size, 1 * PART : 2 * PART] = even[:, :PART] - odd[:, :PART]
    spec[:size, 2 * PART : 3 * PART] = even[:, PART:] + odd[:, PART:]
    spec[:size, 3 * PART : 4 * PART] = even[:, PART:] - odd[:, PART:]
    cos, sin = twiddle[0], twiddle[1]
    first = lax.broadcasted_iota(jnp.int32, (8, WIDTH), 0) == 0
    ends = spec[base:size]
    ends = ends[:, :WIDTH] * twiddle[3, 0:1] + ends[:, WIDTH:] * twiddle[3, 1:2]
    for pair in range(count // 2):
        sides = []
        for k in range(2):
            n = pair * 2 + k
            piece = spec[n * HALF : (n + 1) * HALF]
            re, im = piece[:, :WIDTH], piece[:, WIDTH:]
            im, re = im * cos - re * sin, re * cos + im * sin
            top = jnp.where(first, jnp.broadcast_to(ends[n : n + 1], (8, WIDTH)), im[:8])
            sides.append(jnp.concatenate([re, top, im[8:]], 0))
        high, low = split(jnp.concatenate(sides, 1))
        store(pair * 2, dot(back[...], jnp.concatenate([high, high, low], 0)))


def store_pair(ref, first, value):
    for k in range(4):
        n = first + k // 2
        row = ((n % 4) * 5 + n // 4) * 2 + k % 2
        ref[pl.ds(row, ACROSS, stride=40), :] = value[:, k * 128 : (k + 1) * 128]


def grads_kernel(got, across, back, twiddle, table, out, spec, stage_hi, stage_lo, ends, extra):
    load = functools.partial(load_pair, got)
    spectra_of(load, 36, across, twiddle, table, stage_hi, stage_lo, ends, spec)
    for tail in (False, True):

        def take(n):
            rows = spec[36 * HALF + n : 36 * HALF + n + 1] if tail else spec[n * HALF : (n + 1) * HALF]
            return rows[:, :WIDTH], rows[:, WIDTH:]

        def put(n, re, im):
            rows = jnp.concatenate([re, im], 1)
            if tail:
                extra[n : n + 1] = rows
            else:
                high, low = split(rows)
                stage_hi[n * HALF : (n + 1) * HALF] = high
                stage_lo[n * HALF : (n + 1) * HALF] = low

        crosses = []
        for s in range(4):
            own, other = take(16 + s), take(19 - s)
            er, ei = own[0] + other[0], own[1] - other[1]
            re = im = 0.0
            for b in range(4):
                n = b * 4 + s
                (cr, ci), (xr, xi) = take(n), take(20 + n)
                put(n, er * cr + ei * ci, ei * cr - er * ci)
                re = re + (cr * xr + ci * xi)
                im = im + (cr * xi - ci * xr)
            crosses.append((re, im))
        for s in range(4):
            a, b = crosses[s], crosses[3 - s]
            put(16 + s, a[0] + b[0], a[1] - b[1])
    high, low = split(extra[...])
    stage_hi[20 * HALF : 20 * HALF + 32] = high
    stage_lo[20 * HALF : 20 * HALF + 32] = low
    positions_of(
        20, back, twiddle, table, stage_hi, stage_lo, spec, functools.partial(store_pair, out)
    )


def call(kernel, outs, scratch, flops, *args, in_specs=None, out_specs=None, vmem=VMEM, near=False):
    moved = sum(a.size * a.dtype.itemsize for a in args) + sum(4 * math.prod(o) for o in outs)
    options = dict(in_specs=in_specs) if in_specs else {}
    if out_specs:
        options["out_specs"] = out_specs
    return pl.pallas_call(
        kernel,
        out_shape=[(pltpu.VMEM if near else jax.ShapeDtypeStruct)(o, F32) for o in outs],
        scratch_shapes=scratch,
        compiler_params=pltpu.CompilerParams(vmem_limit_bytes=vmem),
        cost_estimate=pl.CostEstimate(flops=flops, bytes_accessed=moved, transcendentals=0),
        **options,
    )(*args)


def exchange(value, units):
    blocks = value.reshape(DEVICES, units, 2, 128)
    return lax.all_to_all(blocks, ("ctx", "ch"), 0, 0, tiled=True).reshape(-1, 128)


def body(inputs, cotangent, filters):
    across, back, twiddle, table = [jnp.asarray(t) for t in tables()]
    far = pl.BlockSpec(memory_space=pltpu.HBM)
    (packed,) = call(
        pack_kernel,
        [(DEVICES * 18, 128)],
        [pltpu.VMEM((9, WIDTH, WIDTH), F32), pltpu.SemaphoreType.DMA((9,))],
        10**9,
        cotangent, filters, inputs,
        in_specs=[far] * 3,
        vmem=PACK_VMEM,
        near=True,
    )
    got = exchange(packed, 9)
    (grads,) = call(
        grads_kernel,
        [(DEVICES * 10, 128)],
        [pltpu.VMEM((36 * HALF + 48, 2 * WIDTH), F32)]
        + [pltpu.VMEM((36 * HALF + 48, 2 * WIDTH), BF)] * 2
        + [pltpu.VMEM((48, WIDTH), F32), pltpu.VMEM((32, 2 * WIDTH), F32)],
        8 * 10**9,
        got, across, back, twiddle, table,
    )
    return tuple(
        call(
            unpack_kernel,
            [(4, WIDTH, WIDTH), (WIDTH, WIDTH)],
            [pltpu.VMEM((5, WIDTH, WIDTH), F32), pltpu.SemaphoreType.DMA((5,))],
            10**9,
            exchange(grads, 5),
            out_specs=[far] * 2,
        )
    )


def solution(mesh):
    in_specs = (P(None, "ctx", "ch"), P(None, "ctx", "ch"), P("ctx", "ch"))
    out_specs = (P(None, "ctx", "ch"), P("ctx", "ch"))
    return jax.shard_map(body, mesh=mesh, in_specs=in_specs, out_specs=out_specs, check_vma=False)
```

```python
import functools
import math

import jax
import jax.numpy as jnp
import numpy as np
from jax import lax
from jax.experimental import pallas as pl
from jax.experimental.pallas import tpu as pltpu
from jax.sharding import PartitionSpec as P

BF = jnp.bfloat16
F32 = jnp.float32
ACROSS = 64
DEVICES = 256
WIDTH = 256
PART = WIDTH // 2
PERIOD = ACROSS * WIDTH
HALF = ACROSS // 2
FACTOR = 1.0 / (PERIOD * math.sqrt(2.0 * PERIOD))
AHEAD = 7
VMEM = 48 * 1024 * 1024
PACK_VMEM = 56 * 1024 * 1024


def two_parts(table):
    high = np.asarray(table, np.float32).astype(jnp.bfloat16)
    low = (table - high.astype(np.float64)).astype(np.float32).astype(jnp.bfloat16)
    return high, low


def tables():
    p = np.arange(HALF)
    i = np.arange(ACROSS)
    angle = 2.0 * np.pi * (np.outer(p, i) % ACROSS) / ACROSS
    cos, sin = np.cos(angle), np.sin(angle)
    last = np.cos(np.pi * i)
    fore = np.concatenate([cos, -sin], 0)
    fore[HALF] = last
    high, low = two_parts(fore)
    across = np.concatenate([high, low, high], 1)
    weight = np.where(p == 0, 1.0, 2.0)[:, None] * FACTOR
    back = np.concatenate([cos * weight, sin * weight], 0)
    back[HALF] = last * FACTOR
    high, low = two_parts(back.T)
    back = np.concatenate([high, low, high], 1)
    j = np.arange(WIDTH)
    turn = 2.0 * np.pi * np.outer(np.arange(HALF + 1), j) / PERIOD
    c, s = np.cos(turn), np.sin(turn)
    masked = c[:HALF] * (p > 0)[:, None]
    ends = np.zeros((HALF, WIDTH))
    ends[0], ends[1] = c[HALF], s[HALF]
    twiddle = np.stack([c[:HALF], s[:HALF], masked, ends]).astype(np.float32)
    j = np.arange(PART)
    parts = []
    for turns in (2 * np.outer(j, j), np.outer(j, 2 * j + 1), np.outer(2 * j + 1, j)):
        spin = 2.0 * np.pi * (turns % WIDTH) / WIDTH
        c, s = np.cos(spin), np.sin(spin)
        high, low = two_parts(np.block([[c, -s], [s, c]]))
        parts.append(np.concatenate([high, high, low], 0))
    return across, back, twiddle, np.stack(parts)


def split(value):
    high = value.astype(BF)
    return high, (value - high.astype(F32)).astype(BF)


def dot(left, right):
    return jnp.dot(left, right, preferred_element_type=F32)


def mirrored(value):
    back = 7 - lax.broadcasted_iota(jnp.int32, (8, 128), 0)
    columns = []
    for half in range(2):
        lanes = slice(half * 128, (half + 1) * 128)
        groups = [value[k * 8 : (k + 1) * 8, lanes] for k in reversed(range(value.shape[0] // 8))]
        columns.append(
            jnp.concatenate([jnp.take_along_axis(group, back, axis=0) for group in groups], 0)
        )
    return jnp.concatenate(columns, 1)


def both_halves(run):
    upper = lax.axis_index("ch") >= 2
    pl.when(upper)(functools.partial(run, mirrored))
    pl.when(jnp.logical_not(upper))(functools.partial(run, lambda value: value))


def pack_kernel(cotangent, filters, inputs, out, held, sems):
    blocks = [cotangent.at[b] for b in range(4)] + [filters] + [inputs.at[b] for b in range(4)]
    copies = [pltpu.make_async_copy(block, held.at[u], sems.at[u]) for u, block in enumerate(blocks)]
    for copy in copies[:AHEAD]:
        copy.start()

    def run(order):
        for u, copy in enumerate(copies):
            copy.wait()
            if u + AHEAD < len(copies):
                copies[u + AHEAD].start()
            turned = order(held[u].T)
            for half in range(2):
                out[pl.ds(u * 2 + half, DEVICES, stride=18), :] = turned[
                    :, half * 128 : (half + 1) * 128
                ]

    both_halves(run)


def unpack_kernel(ref, inputs, filters, held, sems):
    blocks = [inputs.at[b] for b in range(4)] + [filters]
    copies = [pltpu.make_async_copy(held.at[u], block, sems.at[u]) for u, block in enumerate(blocks)]

    def run(order):
        for u, copy in enumerate(copies):
            halves = [ref[pl.ds(u * 2 + half, DEVICES, stride=10), :] for half in range(2)]
            held[u] = order(jnp.concatenate(halves, 1)).T
            copy.start()
        for copy in copies:
            copy.wait()

    both_halves(run)


def load_pair(ref, first):
    pieces = []
    for n in (first, first + 1):
        for half in range(2):
            row = ((n % 4) * 9 + n // 4) * 2 + half
            pieces.append(ref[pl.ds(row, ACROSS, stride=72), :])
    return jnp.concatenate(pieces, 1)


def spin_rows(high, low, table, odd):
    results = []
    for k, which in enumerate((0, odd)):
        h = jnp.concatenate([high[:, k * PART : (k + 1) * PART], high[:, (k + 2) * PART : (k + 3) * PART]], 1)
        l = jnp.concatenate([low[:, k * PART : (k + 1) * PART], low[:, (k + 2) * PART : (k + 3) * PART]], 1)
        results.append(dot(jnp.concatenate([h, l, h], 1), table[which]))
    return results


def shares(size, parts):
    step = size // parts
    return [slice(at, at + step) for at in range(0, size, step)]


def butterfly(value):
    a, b = value[:, :PART], value[:, PART:]
    return [a + b, a - b]


def spectra_of(load, count, across, twiddle, table, stage_hi, stage_lo, ends, spec):
    cos, sin, masked = twiddle[0], twiddle[1], twiddle[2]
    for pair in range(count // 2):
        high, low = split(load(pair * 2))
        part = dot(across[...], jnp.concatenate([high, high, low], 0))
        turned = []
        for k in range(2):
            re = part[:HALF, k * WIDTH : (k + 1) * WIDTH]
            im = part[HALF:, k * WIDTH : (k + 1) * WIDTH]
            ends[pair * 2 + k : pair * 2 + k + 1, :] = im[:1]
            re, im = re * cos + im * sin, im * masked - re * sin
            turned.append(jnp.concatenate(butterfly(re) + butterfly(im), 1))
        high, low = split(jnp.concatenate(turned, 0))
        stage_hi[pair * 64 : pair * 64 + 64] = high
        stage_lo[pair * 64 : pair * 64 + 64] = low
    base, more = count * HALF, ends.shape[0]
    last = ends[...]
    pieces = butterfly(last * twiddle[3, 0:1]) + butterfly(-last * twiddle[3, 1:2])
    high, low = split(jnp.concatenate(pieces, 1))
    stage_hi[base : base + more] = high
    stage_lo[base : base + more] = low
    for rows in shares(base + more, 3):
        even, odd = spin_rows(stage_hi[rows], stage_lo[rows], table, 1)
        spec[rows, 0 * PART : 1 * PART] = even[:, :PART]
        spec[rows, 1 * PART : 2 * PART] = odd[:, :PART]
        spec[rows, 2 * PART : 3 * PART] = even[:, PART:]
        spec[rows, 3 * PART : 4 * PART] = odd[:, PART:]


def positions_of(count, back, twiddle, table, stage_hi, stage_lo, spec, store):
    base = count * HALF
    size = base + 32
    for rows in shares(size, 2):
        even, odd = spin_rows(stage_hi[rows], stage_lo[rows], table, 2)
        spec[rows, 0 * PART : 1 * PART] = even[:, :PART] + odd[:, :PART]
        spec[rows, 1 * PART : 2 * PART] = even[:, :PART] - odd[:, :PART]
        spec[rows, 2 * PART : 3 * PART] = even[:, PART:] + odd[:, PART:]
        spec[rows, 3 * PART : 4 * PART] = even[:, PART:] - odd[:, PART:]
    cos, sin = twiddle[0], twiddle[1]
    first = lax.broadcasted_iota(jnp.int32, (8, WIDTH), 0) == 0
    ends = spec[base:size]
    ends = ends[:, :WIDTH] * twiddle[3, 0:1] + ends[:, WIDTH:] * twiddle[3, 1:2]
    for pair in range(count // 2):
        sides = []
        for k in range(2):
            n = pair * 2 + k
            piece = spec[n * HALF : (n + 1) * HALF]
            re, im = piece[:, :WIDTH], piece[:, WIDTH:]
            im, re = im * cos - re * sin, re * cos + im * sin
            top = jnp.where(first, jnp.broadcast_to(ends[n : n + 1], (8, WIDTH)), im[:8])
            sides.append(jnp.concatenate([re, top, im[8:]], 0))
        high, low = split(jnp.concatenate(sides, 1))
        store(pair * 2, dot(back[...], jnp.concatenate([high, high, low], 0)))


def store_pair(ref, first, value):
    for k in range(4):
        n = first + k // 2
        row = ((n % 4) * 5 + n // 4) * 2 + k % 2
        ref[pl.ds(row, ACROSS, stride=40), :] = value[:, k * 128 : (k + 1) * 128]


def grads_kernel(got, across, back, twiddle, table, out, spec, stage_hi, stage_lo, ends, extra):
    load = functools.partial(load_pair, got)
    spectra_of(load, 36, across, twiddle, table, stage_hi, stage_lo, ends, spec)
    for tail in (False, True):

        def take(n):
            rows = spec[36 * HALF + n : 36 * HALF + n + 1] if tail else spec[n * HALF : (n + 1) * HALF]
            return rows[:, :WIDTH], rows[:, WIDTH:]

        def put(n, re, im):
            rows = jnp.concatenate([re, im], 1)
            if tail:
                extra[n : n + 1] = rows
            else:
                high, low = split(rows)
                stage_hi[n * HALF : (n + 1) * HALF] = high
                stage_lo[n * HALF : (n + 1) * HALF] = low

        crosses = []
        for s in range(4):
            own, other = take(16 + s), take(19 - s)
            er, ei = own[0] + other[0], own[1] - other[1]
            re = im = 0.0
            for b in range(4):
                n = b * 4 + s
                (cr, ci), (xr, xi) = take(n), take(20 + n)
                put(n, er * cr + ei * ci, ei * cr - er * ci)
                re = re + (cr * xr + ci * xi)
                im = im + (cr * xi - ci * xr)
            crosses.append((re, im))
        for s in range(4):
            a, b = crosses[s], crosses[3 - s]
            put(16 + s, a[0] + b[0], a[1] - b[1])
    high, low = split(extra[...])
    stage_hi[20 * HALF : 20 * HALF + 32] = high
    stage_lo[20 * HALF : 20 * HALF + 32] = low
    positions_of(
        20, back, twiddle, table, stage_hi, stage_lo, spec, functools.partial(store_pair, out)
    )


def call(kernel, outs, scratch, flops, *args, in_specs=None, out_specs=None, vmem=VMEM, near=False):
    moved = sum(a.size * a.dtype.itemsize for a in args) + sum(4 * math.prod(o) for o in outs)
    options = dict(in_specs=in_specs) if in_specs else {}
    if out_specs:
        options["out_specs"] = out_specs
    return pl.pallas_call(
        kernel,
        out_shape=[(pltpu.VMEM if near else jax.ShapeDtypeStruct)(o, F32) for o in outs],
        scratch_shapes=scratch,
        compiler_params=pltpu.CompilerParams(vmem_limit_bytes=vmem),
        cost_estimate=pl.CostEstimate(flops=flops, bytes_accessed=moved, transcendentals=0),
        **options,
    )(*args)


def exchange(value, units):
    blocks = value.reshape(DEVICES, units, 2, 128)
    return lax.all_to_all(blocks, ("ctx", "ch"), 0, 0, tiled=True).reshape(-1, 128)


def body(inputs, cotangent, filters):
    across, back, twiddle, table = [jnp.asarray(t) for t in tables()]
    far = pl.BlockSpec(memory_space=pltpu.HBM)
    (packed,) = call(
        pack_kernel,
        [(DEVICES * 18, 128)],
        [pltpu.VMEM((9, WIDTH, WIDTH), F32), pltpu.SemaphoreType.DMA((9,))],
        10**9,
        cotangent, filters, inputs,
        in_specs=[far] * 3,
        vmem=PACK_VMEM,
        near=True,
    )
    got = exchange(packed, 9)
    (grads,) = call(
        grads_kernel,
        [(DEVICES * 10, 128)],
        [pltpu.VMEM((36 * HALF + 48, 2 * WIDTH), F32)]
        + [pltpu.VMEM((36 * HALF + 48, 2 * WIDTH), BF)] * 2
        + [pltpu.VMEM((48, WIDTH), F32), pltpu.VMEM((32, 2 * WIDTH), F32)],
        8 * 10**9,
        got, across, back, twiddle, table,
    )
    return tuple(
        call(
            unpack_kernel,
            [(4, WIDTH, WIDTH), (WIDTH, WIDTH)],
            [pltpu.VMEM((5, WIDTH, WIDTH), F32), pltpu.SemaphoreType.DMA((5,))],
            10**9,
            exchange(grads, 5),
            out_specs=[far] * 2,
        )
    )


def solution(mesh):
    in_specs = (P(None, "ctx", "ch"), P(None, "ctx", "ch"), P("ctx", "ch"))
    out_specs = (P(None, "ctx", "ch"), P("ctx", "ch"))
    return jax.shard_map(body, mesh=mesh, in_specs=in_specs, out_specs=out_specs, check_vma=False)
```

```python
import functools
import math

import jax
import jax.numpy as jnp
import numpy as np
from jax import lax
from jax.experimental import pallas as pl
from jax.experimental.pallas import tpu as pltpu
from jax.sharding import PartitionSpec as P

BF = jnp.bfloat16
F32 = jnp.float32
ACROSS = 64
GROUP = 2 * ACROSS
WIDTH = 256
PART = WIDTH // 2
PERIOD = ACROSS * WIDTH
HALF = ACROSS // 2
FACTOR = 1.0 / (PERIOD * math.sqrt(2.0 * PERIOD))
AHEAD = 7
VMEM = 48 * 1024 * 1024
PACK_VMEM = 56 * 1024 * 1024


def two_parts(table):
    high = np.asarray(table, np.float32).astype(jnp.bfloat16)
    low = (table - high.astype(np.float64)).astype(np.float32).astype(jnp.bfloat16)
    return high, low


def tables():
    p = np.arange(HALF)
    i = np.arange(ACROSS)
    angle = 2.0 * np.pi * (np.outer(p, i) % ACROSS) / ACROSS
    cos, sin = np.cos(angle), np.sin(angle)
    last = np.cos(np.pi * i)
    fore = np.concatenate([cos, -sin], 0)
    fore[HALF] = last
    high, low = two_parts(fore)
    across = np.concatenate([high, low, high], 1)
    weight = np.where(p == 0, 1.0, 2.0)[:, None] * FACTOR
    back = np.concatenate([cos * weight, sin * weight], 0)
    back[HALF] = last * FACTOR
    high, low = two_parts(back.T)
    back = np.concatenate([high, low, high], 1)
    j = np.arange(WIDTH)
    turn = 2.0 * np.pi * np.outer(np.arange(HALF + 1), j) / PERIOD
    c, s = np.cos(turn), np.sin(turn)
    masked = c[:HALF] * (p > 0)[:, None]
    ends = np.zeros((HALF, WIDTH))
    ends[0], ends[1] = c[HALF], s[HALF]
    twiddle = np.stack([c[:HALF], s[:HALF], masked, ends]).astype(np.float32)
    j = np.arange(PART)
    parts = []
    for turns in (2 * np.outer(j, j), np.outer(j, 2 * j + 1), np.outer(2 * j + 1, j)):
        spin = 2.0 * np.pi * (turns % WIDTH) / WIDTH
        c, s = np.cos(spin), np.sin(spin)
        high, low = two_parts(np.block([[c, -s], [s, c]]))
        parts.append(np.concatenate([high, high, low], 0))
    return across, back, twiddle, np.stack(parts)


def split(value):
    high = value.astype(BF)
    return high, (value - high.astype(F32)).astype(BF)


def dot(left, right):
    return jnp.dot(left, right, preferred_element_type=F32)


def mirrored(value):
    back = 7 - lax.broadcasted_iota(jnp.int32, (8, 128), 0)
    columns = []
    for half in range(2):
        lanes = slice(half * 128, (half + 1) * 128)
        groups = [value[k * 8 : (k + 1) * 8, lanes] for k in reversed(range(value.shape[0] // 8))]
        columns.append(
            jnp.concatenate([jnp.take_along_axis(group, back, axis=0) for group in groups], 0)
        )
    return jnp.concatenate(columns, 1)


def both_halves(run):
    upper = lax.axis_index("ch") >= 2
    pl.when(upper)(functools.partial(run, mirrored))
    pl.when(jnp.logical_not(upper))(functools.partial(run, lambda value: value))


def pack_kernel(cotangent, filters, inputs, out, held, sems):
    blocks = [cotangent.at[b] for b in range(4)] + [filters] + [inputs.at[b] for b in range(4)]
    copies = [pltpu.make_async_copy(block, held.at[u], sems.at[u]) for u, block in enumerate(blocks)]
    for copy in copies[:AHEAD]:
        copy.start()

    def run(order):
        for u, copy in enumerate(copies):
            copy.wait()
            if u + AHEAD < len(copies):
                copies[u + AHEAD].start()
            turned = order(held[u].T)
            for k in range(4):
                out[pl.ds(u * 4 + k, GROUP, stride=36), :] = turned[
                    k // 2 * GROUP : (k // 2 + 1) * GROUP, k % 2 * 128 : (k % 2 + 1) * 128
                ]

    both_halves(run)


def unpack_kernel(ref, inputs, filters, held, sems):
    blocks = [inputs.at[b] for b in range(4)] + [filters]
    copies = [pltpu.make_async_copy(held.at[u], block, sems.at[u]) for u, block in enumerate(blocks)]

    def run(order):
        for u, copy in enumerate(copies):
            parts = [ref[pl.ds(u * 4 + k, GROUP, stride=20), :] for k in range(4)]
            sides = [jnp.concatenate(parts[k : k + 2], 1) for k in (0, 2)]
            held[u] = order(jnp.concatenate(sides, 0)).T
            copy.start()
        for copy in copies:
            copy.wait()

    both_halves(run)


def row_of(n, half, units):
    side, slot = ((0, 0), (0, 1), (1, 1), (1, 0))[n % 4]
    return ((side * units + n // 4) * 2 + slot) * 2 + half


def load_pair(ref, first):
    pieces = []
    for n in (first, first + 1):
        for half in range(2):
            pieces.append(ref[pl.ds(row_of(n, half, 9), ACROSS, stride=72), :])
    return jnp.concatenate(pieces, 1)


def spin_rows(high, low, table, odd):
    results = []
    for k, which in enumerate((0, odd)):
        h = jnp.concatenate([high[:, k * PART : (k + 1) * PART], high[:, (k + 2) * PART : (k + 3) * PART]], 1)
        l = jnp.concatenate([low[:, k * PART : (k + 1) * PART], low[:, (k + 2) * PART : (k + 3) * PART]], 1)
        results.append(dot(jnp.concatenate([h, l, h], 1), table[which]))
    return results


def shares(size, parts):
    step = size // parts
    return [slice(at, at + step) for at in range(0, size, step)]


def butterfly(value):
    a, b = value[:, :PART], value[:, PART:]
    return [a + b, a - b]


def spectra_of(load, count, across, twiddle, table, stage_hi, stage_lo, ends, spec):
    cos, sin, masked = twiddle[0], twiddle[1], twiddle[2]
    for pair in range(count // 2):
        high, low = split(load(pair * 2))
        part = dot(across[...], jnp.concatenate([high, high, low], 0))
        turned = []
        for k in range(2):
            re = part[:HALF, k * WIDTH : (k + 1) * WIDTH]
            im = part[HALF:, k * WIDTH : (k + 1) * WIDTH]
            ends[pair * 2 + k : pair * 2 + k + 1, :] = im[:1]
            re, im = re * cos + im * sin, im * masked - re * sin
            turned.append(jnp.concatenate(butterfly(re) + butterfly(im), 1))
        high, low = split(jnp.concatenate(turned, 0))
        stage_hi[pair * 64 : pair * 64 + 64] = high
        stage_lo[pair * 64 : pair * 64 + 64] = low
    base, more = count * HALF, ends.shape[0]
    last = ends[...]
    pieces = butterfly(last * twiddle[3, 0:1]) + butterfly(-last * twiddle[3, 1:2])
    high, low = split(jnp.concatenate(pieces, 1))
    stage_hi[base : base + more] = high
    stage_lo[base : base + more] = low
    for rows in shares(base + more, 3):
        even, odd = spin_rows(stage_hi[rows], stage_lo[rows], table, 1)
        spec[rows, 0 * PART : 1 * PART] = even[:, :PART]
        spec[rows, 1 * PART : 2 * PART] = odd[:, :PART]
        spec[rows, 2 * PART : 3 * PART] = even[:, PART:]
        spec[rows, 3 * PART : 4 * PART] = odd[:, PART:]


def positions_of(count, back, twiddle, table, stage_hi, stage_lo, spec, store):
    base = count * HALF
    size = base + 32
    for rows in shares(size, 2):
        even, odd = spin_rows(stage_hi[rows], stage_lo[rows], table, 2)
        spec[rows, 0 * PART : 1 * PART] = even[:, :PART] + odd[:, :PART]
        spec[rows, 1 * PART : 2 * PART] = even[:, :PART] - odd[:, :PART]
        spec[rows, 2 * PART : 3 * PART] = even[:, PART:] + odd[:, PART:]
        spec[rows, 3 * PART : 4 * PART] = even[:, PART:] - odd[:, PART:]
    cos, sin = twiddle[0], twiddle[1]
    first = lax.broadcasted_iota(jnp.int32, (8, WIDTH), 0) == 0
    ends = spec[base:size]
    ends = ends[:, :WIDTH] * twiddle[3, 0:1] + ends[:, WIDTH:] * twiddle[3, 1:2]
    for pair in range(count // 2):
        sides = []
        for k in range(2):
            n = pair * 2 + k
            piece = spec[n * HALF : (n + 1) * HALF]
            re, im = piece[:, :WIDTH], piece[:, WIDTH:]
            im, re = im * cos - re * sin, re * cos + im * sin
            top = jnp.where(first, jnp.broadcast_to(ends[n : n + 1], (8, WIDTH)), im[:8])
            sides.append(jnp.concatenate([re, top, im[8:]], 0))
        high, low = split(jnp.concatenate(sides, 1))
        store(pair * 2, dot(back[...], jnp.concatenate([high, high, low], 0)))


def store_pair(ref, first, value):
    for k in range(4):
        n = first + k // 2
        ref[pl.ds(row_of(n, k % 2, 5), ACROSS, stride=40), :] = value[:, k * 128 : (k + 1) * 128]


def grads_kernel(got, across, back, twiddle, table, out, spec, stage_hi, stage_lo, ends, extra):
    load = functools.partial(load_pair, got)
    spectra_of(load, 36, across, twiddle, table, stage_hi, stage_lo, ends, spec)
    for tail in (False, True):

        def take(n):
            rows = spec[36 * HALF + n : 36 * HALF + n + 1] if tail else spec[n * HALF : (n + 1) * HALF]
            return rows[:, :WIDTH], rows[:, WIDTH:]

        def put(n, re, im):
            rows = jnp.concatenate([re, im], 1)
            if tail:
                extra[n : n + 1] = rows
            else:
                high, low = split(rows)
                stage_hi[n * HALF : (n + 1) * HALF] = high
                stage_lo[n * HALF : (n + 1) * HALF] = low

        crosses = []
        for s in range(4):
            own, other = take(16 + s), take(19 - s)
            er, ei = own[0] + other[0], own[1] - other[1]
            re = im = 0.0
            for b in range(4):
                n = b * 4 + s
                (cr, ci), (xr, xi) = take(n), take(20 + n)
                put(n, er * cr + ei * ci, ei * cr - er * ci)
                re = re + (cr * xr + ci * xi)
                im = im + (cr * xi - ci * xr)
            crosses.append((re, im))
        for s in range(4):
            a, b = crosses[s], crosses[3 - s]
            put(16 + s, a[0] + b[0], a[1] - b[1])
    high, low = split(extra[...])
    stage_hi[20 * HALF : 20 * HALF + 32] = high
    stage_lo[20 * HALF : 20 * HALF + 32] = low
    positions_of(
        20, back, twiddle, table, stage_hi, stage_lo, spec, functools.partial(store_pair, out)
    )


def call(kernel, outs, scratch, flops, *args, in_specs=None, out_specs=None, vmem=VMEM, near=False):
    moved = sum(a.size * a.dtype.itemsize for a in args) + sum(4 * math.prod(o) for o in outs)
    options = dict(in_specs=in_specs) if in_specs else {}
    if out_specs:
        options["out_specs"] = out_specs
    return pl.pallas_call(
        kernel,
        out_shape=[(pltpu.VMEM if near else jax.ShapeDtypeStruct)(o, F32) for o in outs],
        scratch_shapes=scratch,
        compiler_params=pltpu.CompilerParams(vmem_limit_bytes=vmem),
        cost_estimate=pl.CostEstimate(flops=flops, bytes_accessed=moved, transcendentals=0),
        **options,
    )(*args)


def exchange(value, units):
    groups = [[i * 4 + s for i in range(ACROSS) for s in (low, 3 - low)] for low in range(2)]
    blocks = value.reshape(GROUP, units, 4, 128)
    return lax.all_to_all(
        blocks, ("ctx", "ch"), 0, 0, axis_index_groups=groups, tiled=True
    ).reshape(-1, 128)


def body(inputs, cotangent, filters):
    across, back, twiddle, table = [jnp.asarray(t) for t in tables()]
    far = pl.BlockSpec(memory_space=pltpu.HBM)
    (packed,) = call(
        pack_kernel,
        [(GROUP * 36, 128)],
        [pltpu.VMEM((9, WIDTH, WIDTH), F32), pltpu.SemaphoreType.DMA((9,))],
        10**9,
        cotangent, filters, inputs,
        in_specs=[far] * 3,
        vmem=PACK_VMEM,
        near=True,
    )
    got = exchange(packed, 9)
    (grads,) = call(
        grads_kernel,
        [(GROUP * 20, 128)],
        [pltpu.VMEM((36 * HALF + 48, 2 * WIDTH), F32)]
        + [pltpu.VMEM((36 * HALF + 48, 2 * WIDTH), BF)] * 2
        + [pltpu.VMEM((48, WIDTH), F32), pltpu.VMEM((32, 2 * WIDTH), F32)],
        8 * 10**9,
        got, across, back, twiddle, table,
    )
    return tuple(
        call(
            unpack_kernel,
            [(4, WIDTH, WIDTH), (WIDTH, WIDTH)],
            [pltpu.VMEM((5, WIDTH, WIDTH), F32), pltpu.SemaphoreType.DMA((5,))],
            10**9,
            exchange(grads, 5),
            out_specs=[far] * 2,
        )
    )


def solution(mesh):
    in_specs = (P(None, "ctx", "ch"), P(None, "ctx", "ch"), P("ctx", "ch"))
    out_specs = (P(None, "ctx", "ch"), P("ctx", "ch"))
    return jax.shard_map(body, mesh=mesh, in_specs=in_specs, out_specs=out_specs, check_vma=False)
```

```python
import functools
import math

import jax
import jax.numpy as jnp
import numpy as np
from jax import lax
from jax.experimental import pallas as pl
from jax.experimental.pallas import tpu as pltpu
from jax.sharding import PartitionSpec as P

BF = jnp.bfloat16
F32 = jnp.float32
ACROSS = 64
GROUP = 2 * ACROSS
WIDTH = 256
PART = WIDTH // 2
PERIOD = ACROSS * WIDTH
HALF = ACROSS // 2
FACTOR = 1.0 / (PERIOD * math.sqrt(2.0 * PERIOD))
AHEAD = 14
VMEM = 48 * 1024 * 1024
PACK_VMEM = 56 * 1024 * 1024


def two_parts(table):
    high = np.asarray(table, np.float32).astype(jnp.bfloat16)
    low = (table - high.astype(np.float64)).astype(np.float32).astype(jnp.bfloat16)
    return high, low


def tables():
    p = np.arange(HALF)
    i = np.arange(ACROSS)
    angle = 2.0 * np.pi * (np.outer(p, i) % ACROSS) / ACROSS
    cos, sin = np.cos(angle), np.sin(angle)
    last = np.cos(np.pi * i)
    fore = np.concatenate([cos, -sin], 0)
    fore[HALF] = last
    high, low = two_parts(fore)
    across = np.concatenate([high, low, high], 1)
    weight = np.where(p == 0, 1.0, 2.0)[:, None] * FACTOR
    back = np.concatenate([cos * weight, sin * weight], 0)
    back[HALF] = last * FACTOR
    high, low = two_parts(back.T)
    back = np.concatenate([high, low, high], 1)
    j = np.arange(WIDTH)
    turn = 2.0 * np.pi * np.outer(np.arange(HALF + 1), j) / PERIOD
    c, s = np.cos(turn), np.sin(turn)
    masked = c[:HALF] * (p > 0)[:, None]
    ends = np.zeros((HALF, WIDTH))
    ends[0], ends[1] = c[HALF], s[HALF]
    twiddle = np.stack([c[:HALF], s[:HALF], masked, ends]).astype(np.float32)
    j = np.arange(PART)
    parts = []
    for turns in (2 * np.outer(j, j), np.outer(j, 2 * j + 1), np.outer(2 * j + 1, j)):
        spin = 2.0 * np.pi * (turns % WIDTH) / WIDTH
        c, s = np.cos(spin), np.sin(spin)
        high, low = two_parts(np.block([[c, -s], [s, c]]))
        parts.append(np.concatenate([high, high, low], 0))
    return across, back, twiddle, np.stack(parts)


def split(value):
    high = value.astype(BF)
    return high, (value - high.astype(F32)).astype(BF)


def dot(left, right):
    return jnp.dot(left, right, preferred_element_type=F32)


def mirrored(value):
    back = 7 - lax.broadcasted_iota(jnp.int32, (8, 128), 0)
    groups = [value[k * 8 : (k + 1) * 8] for k in reversed(range(value.shape[0] // 8))]
    return jnp.concatenate([jnp.take_along_axis(group, back, axis=0) for group in groups], 0)


def both_halves(run):
    upper = lax.axis_index("ch") >= 2
    pl.when(upper)(functools.partial(run, mirrored))
    pl.when(jnp.logical_not(upper))(functools.partial(run, lambda value: value))


def half_blocks(stacked, single, count):
    whole = [stacked.at[b] for b in range(count)] + ([single] if single is not None else [])
    return [block.at[pl.ds(half * PART, PART)] for block in whole for half in range(2)]


def pack_kernel(cotangent, filters, inputs, out, held, sems):
    blocks = half_blocks(cotangent, filters, 4) + half_blocks(inputs, None, 4)
    copies = [pltpu.make_async_copy(block, held.at[h], sems.at[h]) for h, block in enumerate(blocks)]
    for copy in copies[:AHEAD]:
        copy.start()

    def run(order):
        for h, copy in enumerate(copies):
            copy.wait()
            if h + AHEAD < len(copies):
                copies[h + AHEAD].start()
            turned = order(held[h].T)
            for slot in range(2):
                row = (h // 2) * 4 + slot * 2 + h % 2
                out[pl.ds(row, GROUP, stride=36), :] = turned[slot * GROUP : (slot + 1) * GROUP]

    both_halves(run)


def unpack_kernel(ref, inputs, filters, held, sems):
    blocks = half_blocks(inputs, filters, 4)
    copies = [pltpu.make_async_copy(held.at[h], block, sems.at[h]) for h, block in enumerate(blocks)]

    def run(order):
        for h, copy in enumerate(copies):
            rows = [(h // 2) * 4 + slot * 2 + h % 2 for slot in range(2)]
            parts = [ref[pl.ds(row, GROUP, stride=20), :] for row in rows]
            held[h] = order(jnp.concatenate(parts, 0)).T
            copy.start()
        for copy in copies:
            copy.wait()

    both_halves(run)


def row_of(n, half, units):
    side, slot = ((0, 0), (0, 1), (1, 1), (1, 0))[n % 4]
    return ((side * units + n // 4) * 2 + slot) * 2 + half


def load_pair(ref, first):
    pieces = []
    for n in (first, first + 1):
        for half in range(2):
            pieces.append(ref[pl.ds(row_of(n, half, 9), ACROSS, stride=72), :])
    return jnp.concatenate(pieces, 1)


def spin_rows(high, low, table, odd):
    results = []
    for k, which in enumerate((0, odd)):
        h = jnp.concatenate([high[:, k * PART : (k + 1) * PART], high[:, (k + 2) * PART : (k + 3) * PART]], 1)
        l = jnp.concatenate([low[:, k * PART : (k + 1) * PART], low[:, (k + 2) * PART : (k + 3) * PART]], 1)
        results.append(dot(jnp.concatenate([h, l, h], 1), table[which]))
    return results


def shares(size, parts):
    step = size // parts
    return [slice(at, at + step) for at in range(0, size, step)]


def butterfly(value):
    a, b = value[:, :PART], value[:, PART:]
    return [a + b, a - b]


def spectra_of(load, count, across, twiddle, table, stage_hi, stage_lo, ends, spec):
    cos, sin, masked = twiddle[0], twiddle[1], twiddle[2]
    for pair in range(count // 2):
        high, low = split(load(pair * 2))
        part = dot(across[...], jnp.concatenate([high, high, low], 0))
        turned = []
        for k in range(2):
            re = part[:HALF, k * WIDTH : (k + 1) * WIDTH]
            im = part[HALF:, k * WIDTH : (k + 1) * WIDTH]
            ends[pair * 2 + k : pair * 2 + k + 1, :] = im[:1]
            re, im = re * cos + im * sin, im * masked - re * sin
            turned.append(jnp.concatenate(butterfly(re) + butterfly(im), 1))
        high, low = split(jnp.concatenate(turned, 0))
        stage_hi[pair * 64 : pair * 64 + 64] = high
        stage_lo[pair * 64 : pair * 64 + 64] = low
    base, more = count * HALF, ends.shape[0]
    last = ends[...]
    pieces = butterfly(last * twiddle[3, 0:1]) + butterfly(-last * twiddle[3, 1:2])
    high, low = split(jnp.concatenate(pieces, 1))
    stage_hi[base : base + more] = high
    stage_lo[base : base + more] = low
    for rows in shares(base + more, 3):
        even, odd = spin_rows(stage_hi[rows], stage_lo[rows], table, 1)
        spec[rows, 0 * PART : 1 * PART] = even[:, :PART]
        spec[rows, 1 * PART : 2 * PART] = odd[:, :PART]
        spec[rows, 2 * PART : 3 * PART] = even[:, PART:]
        spec[rows, 3 * PART : 4 * PART] = odd[:, PART:]


def positions_of(count, back, twiddle, table, stage_hi, stage_lo, spec, store):
    base = count * HALF
    size = base + 32
    for rows in shares(size, 2):
        even, odd = spin_rows(stage_hi[rows], stage_lo[rows], table, 2)
        spec[rows, 0 * PART : 1 * PART] = even[:, :PART] + odd[:, :PART]
        spec[rows, 1 * PART : 2 * PART] = even[:, :PART] - odd[:, :PART]
        spec[rows, 2 * PART : 3 * PART] = even[:, PART:] + odd[:, PART:]
        spec[rows, 3 * PART : 4 * PART] = even[:, PART:] - odd[:, PART:]
    cos, sin = twiddle[0], twiddle[1]
    first = lax.broadcasted_iota(jnp.int32, (8, WIDTH), 0) == 0
    ends = spec[base:size]
    ends = ends[:, :WIDTH] * twiddle[3, 0:1] + ends[:, WIDTH:] * twiddle[3, 1:2]
    for pair in range(count // 2):
        sides = []
        for k in range(2):
            n = pair * 2 + k
            piece = spec[n * HALF : (n + 1) * HALF]
            re, im = piece[:, :WIDTH], piece[:, WIDTH:]
            im, re = im * cos - re * sin, re * cos + im * sin
            top = jnp.where(first, jnp.broadcast_to(ends[n : n + 1], (8, WIDTH)), im[:8])
            sides.append(jnp.concatenate([re, top, im[8:]], 0))
        high, low = split(jnp.concatenate(sides, 1))
        store(pair * 2, dot(back[...], jnp.concatenate([high, high, low], 0)))


def store_pair(ref, first, value):
    for k in range(4):
        n = first + k // 2
        ref[pl.ds(row_of(n, k % 2, 5), ACROSS, stride=40), :] = value[:, k * 128 : (k + 1) * 128]


def grads_kernel(got, across, back, twiddle, table, out, spec, stage_hi, stage_lo, ends, extra):
    load = functools.partial(load_pair, got)
    spectra_of(load, 36, across, twiddle, table, stage_hi, stage_lo, ends, spec)
    for tail in (False, True):

        def take(n):
            rows = spec[36 * HALF + n : 36 * HALF + n + 1] if tail else spec[n * HALF : (n + 1) * HALF]
            return rows[:, :WIDTH], rows[:, WIDTH:]

        def put(n, re, im):
            rows = jnp.concatenate([re, im], 1)
            if tail:
                extra[n : n + 1] = rows
            else:
                high, low = split(rows)
                stage_hi[n * HALF : (n + 1) * HALF] = high
                stage_lo[n * HALF : (n + 1) * HALF] = low

        crosses = []
        for s in range(4):
            own, other = take(16 + s), take(19 - s)
            er, ei = own[0] + other[0], own[1] - other[1]
            re = im = 0.0
            for b in range(4):
                n = b * 4 + s
                (cr, ci), (xr, xi) = take(n), take(20 + n)
                put(n, er * cr + ei * ci, ei * cr - er * ci)
                re = re + (cr * xr + ci * xi)
                im = im + (cr * xi - ci * xr)
            crosses.append((re, im))
        for s in range(4):
            a, b = crosses[s], crosses[3 - s]
            put(16 + s, a[0] + b[0], a[1] - b[1])
    high, low = split(extra[...])
    stage_hi[20 * HALF : 20 * HALF + 32] = high
    stage_lo[20 * HALF : 20 * HALF + 32] = low
    positions_of(
        20, back, twiddle, table, stage_hi, stage_lo, spec, functools.partial(store_pair, out)
    )


def call(kernel, outs, scratch, flops, *args, in_specs=None, out_specs=None, vmem=VMEM, near=False):
    moved = sum(a.size * a.dtype.itemsize for a in args) + sum(4 * math.prod(o) for o in outs)
    options = dict(in_specs=in_specs) if in_specs else {}
    if out_specs:
        options["out_specs"] = out_specs
    return pl.pallas_call(
        kernel,
        out_shape=[(pltpu.VMEM if near else jax.ShapeDtypeStruct)(o, F32) for o in outs],
        scratch_shapes=scratch,
        compiler_params=pltpu.CompilerParams(vmem_limit_bytes=vmem),
        cost_estimate=pl.CostEstimate(flops=flops, bytes_accessed=moved, transcendentals=0),
        **options,
    )(*args)


def exchange(value, units):
    groups = [[i * 4 + s for i in range(ACROSS) for s in (low, 3 - low)] for low in range(2)]
    blocks = value.reshape(GROUP, units, 4, 128)
    return lax.all_to_all(
        blocks, ("ctx", "ch"), 0, 0, axis_index_groups=groups, tiled=True
    ).reshape(-1, 128)


def body(inputs, cotangent, filters):
    across, back, twiddle, table = [jnp.asarray(t) for t in tables()]
    far = pl.BlockSpec(memory_space=pltpu.HBM)
    (packed,) = call(
        pack_kernel,
        [(GROUP * 36, 128)],
        [pltpu.VMEM((18, PART, WIDTH), F32), pltpu.SemaphoreType.DMA((18,))],
        10**9,
        cotangent, filters, inputs,
        in_specs=[far] * 3,
        vmem=PACK_VMEM,
        near=True,
    )
    got = exchange(packed, 9)
    (grads,) = call(
        grads_kernel,
        [(GROUP * 20, 128)],
        [pltpu.VMEM((36 * HALF + 48, 2 * WIDTH), F32)]
        + [pltpu.VMEM((36 * HALF + 48, 2 * WIDTH), BF)] * 2
        + [pltpu.VMEM((48, WIDTH), F32), pltpu.VMEM((32, 2 * WIDTH), F32)],
        8 * 10**9,
        got, across, back, twiddle, table,
    )
    return tuple(
        call(
            unpack_kernel,
            [(4, WIDTH, WIDTH), (WIDTH, WIDTH)],
            [pltpu.VMEM((10, PART, WIDTH), F32), pltpu.SemaphoreType.DMA((10,))],
            10**9,
            exchange(grads, 5),
            out_specs=[far] * 2,
        )
    )


def solution(mesh):
    in_specs = (P(None, "ctx", "ch"), P(None, "ctx", "ch"), P("ctx", "ch"))
    out_specs = (P(None, "ctx", "ch"), P("ctx", "ch"))
    return jax.shard_map(body, mesh=mesh, in_specs=in_specs, out_specs=out_specs, check_vma=False)
```

```python
import functools
import math

import jax
import jax.numpy as jnp
import numpy as np
from jax import lax
from jax.experimental import pallas as pl
from jax.experimental.pallas import tpu as pltpu
from jax.sharding import PartitionSpec as P

BF = jnp.bfloat16
F32 = jnp.float32
ACROSS = 64
GROUP = 2 * ACROSS
WIDTH = 256
PART = WIDTH // 2
PERIOD = ACROSS * WIDTH
HALF = ACROSS // 2
FACTOR = 1.0 / (PERIOD * math.sqrt(2.0 * PERIOD))
VMEM = 48 * 1024 * 1024
PACK_VMEM = 56 * 1024 * 1024


def two_parts(table):
    high = np.asarray(table, np.float32).astype(jnp.bfloat16)
    low = (table - high.astype(np.float64)).astype(np.float32).astype(jnp.bfloat16)
    return high, low


def tables():
    p = np.arange(HALF)
    i = np.arange(ACROSS)
    angle = 2.0 * np.pi * (np.outer(p, i) % ACROSS) / ACROSS
    cos, sin = np.cos(angle), np.sin(angle)
    last = np.cos(np.pi * i)
    fore = np.concatenate([cos, -sin], 0)
    fore[HALF] = last
    high, low = two_parts(fore)
    across = np.concatenate([high, low, high], 1)
    weight = np.where(p == 0, 1.0, 2.0)[:, None] * FACTOR
    back = np.concatenate([cos * weight, sin * weight], 0)
    back[HALF] = last * FACTOR
    high, low = two_parts(back.T)
    back = np.concatenate([high, low, high], 1)
    j = np.arange(WIDTH)
    turn = 2.0 * np.pi * np.outer(np.arange(HALF + 1), j) / PERIOD
    c, s = np.cos(turn), np.sin(turn)
    masked = c[:HALF] * (p > 0)[:, None]
    ends = np.zeros((HALF, WIDTH))
    ends[0], ends[1] = c[HALF], s[HALF]
    twiddle = np.stack([c[:HALF], s[:HALF], masked, ends]).astype(np.float32)
    j = np.arange(PART)
    parts = []
    for turns in (2 * np.outer(j, j), np.outer(j, 2 * j + 1), np.outer(2 * j + 1, j)):
        spin = 2.0 * np.pi * (turns % WIDTH) / WIDTH
        c, s = np.cos(spin), np.sin(spin)
        high, low = two_parts(np.block([[c, -s], [s, c]]))
        parts.append(np.concatenate([high, high, low], 0))
    return across, back, twiddle, np.stack(parts)


def split(value):
    high = value.astype(BF)
    return high, (value - high.astype(F32)).astype(BF)


def dot(left, right):
    return jnp.dot(left, right, preferred_element_type=F32)


def mirrored(value):
    back = 7 - lax.broadcasted_iota(jnp.int32, (8, 128), 0)
    columns = []
    for half in range(2):
        lanes = slice(half * 128, (half + 1) * 128)
        groups = [value[k * 8 : (k + 1) * 8, lanes] for k in reversed(range(value.shape[0] // 8))]
        columns.append(
            jnp.concatenate([jnp.take_along_axis(group, back, axis=0) for group in groups], 0)
        )
    return jnp.concatenate(columns, 1)


def both_halves(run):
    upper = lax.axis_index("ch") >= 2
    pl.when(upper)(functools.partial(run, mirrored))
    pl.when(jnp.logical_not(upper))(functools.partial(run, lambda value: value))


def pack_kernel(cotangent, filters, inputs, out, held, sems):
    pieces = [((4,), filters, held.at[4])]
    for base, source in ((0, cotangent), (5, inputs)):
        for b in (0, 2):
            pair = (base + b, base + b + 1)
            pieces.append((pair, source.at[pl.ds(b, 2)], held.at[pl.ds(base + b, 2)]))
    copies = [
        pltpu.make_async_copy(source, target, sems.at[k])
        for k, (_, source, target) in enumerate(pieces)
    ]
    for copy in copies:
        copy.start()

    def run(order):
        for copy, (units, _, _) in zip(copies, pieces):
            copy.wait()
            for u in units:
                turned = order(held[u].T)
                for k in range(4):
                    out[pl.ds(u * 4 + k, GROUP, stride=36), :] = turned[
                        k // 2 * GROUP : (k // 2 + 1) * GROUP, k % 2 * 128 : (k % 2 + 1) * 128
                    ]

    both_halves(run)


def unpack_kernel(ref, inputs, filters, held, sems):
    blocks = [inputs.at[b] for b in range(4)] + [filters]
    copies = [pltpu.make_async_copy(held.at[u], block, sems.at[u]) for u, block in enumerate(blocks)]

    def run(order):
        for u, copy in enumerate(copies):
            parts = [ref[pl.ds(u * 4 + k, GROUP, stride=20), :] for k in range(4)]
            sides = [jnp.concatenate(parts[k : k + 2], 1) for k in (0, 2)]
            held[u] = order(jnp.concatenate(sides, 0)).T
            copy.start()
        for copy in copies:
            copy.wait()

    both_halves(run)


def row_of(n, half, units):
    side, slot = ((0, 0), (0, 1), (1, 1), (1, 0))[n % 4]
    return ((side * units + n // 4) * 2 + slot) * 2 + half


def load_pair(ref, first):
    pieces = []
    for n in (first, first + 1):
        for half in range(2):
            pieces.append(ref[pl.ds(row_of(n, half, 9), ACROSS, stride=72), :])
    return jnp.concatenate(pieces, 1)


def spin_rows(high, low, table, odd):
    results = []
    for k, which in enumerate((0, odd)):
        h = jnp.concatenate([high[:, k * PART : (k + 1) * PART], high[:, (k + 2) * PART : (k + 3) * PART]], 1)
        l = jnp.concatenate([low[:, k * PART : (k + 1) * PART], low[:, (k + 2) * PART : (k + 3) * PART]], 1)
        results.append(dot(jnp.concatenate([h, l, h], 1), table[which]))
    return results


def shares(size, parts):
    step = size // parts
    return [slice(at, at + step) for at in range(0, size, step)]


def butterfly(value):
    a, b = value[:, :PART], value[:, PART:]
    return [a + b, a - b]


def spectra_of(load, count, across, twiddle, table, stage_hi, stage_lo, ends, spec):
    cos, sin, masked = twiddle[0], twiddle[1], twiddle[2]
    for pair in range(count // 2):
        high, low = split(load(pair * 2))
        part = dot(across[...], jnp.concatenate([high, high, low], 0))
        turned = []
        for k in range(2):
            re = part[:HALF, k * WIDTH : (k + 1) * WIDTH]
            im = part[HALF:, k * WIDTH : (k + 1) * WIDTH]
            ends[pair * 2 + k : pair * 2 + k + 1, :] = im[:1]
            re, im = re * cos + im * sin, im * masked - re * sin
            turned.append(jnp.concatenate(butterfly(re) + butterfly(im), 1))
        high, low = split(jnp.concatenate(turned, 0))
        stage_hi[pair * 64 : pair * 64 + 64] = high
        stage_lo[pair * 64 : pair * 64 + 64] = low
    base, more = count * HALF, ends.shape[0]
    last = ends[...]
    pieces = butterfly(last * twiddle[3, 0:1]) + butterfly(-last * twiddle[3, 1:2])
    high, low = split(jnp.concatenate(pieces, 1))
    stage_hi[base : base + more] = high
    stage_lo[base : base + more] = low
    for rows in shares(base + more, 3):
        even, odd = spin_rows(stage_hi[rows], stage_lo[rows], table, 1)
        spec[rows, 0 * PART : 1 * PART] = even[:, :PART]
        spec[rows, 1 * PART : 2 * PART] = odd[:, :PART]
        spec[rows, 2 * PART : 3 * PART] = even[:, PART:]
        spec[rows, 3 * PART : 4 * PART] = odd[:, PART:]


def positions_of(count, back, twiddle, table, stage_hi, stage_lo, spec, store):
    base = count * HALF
    size = base + 32
    for rows in shares(size, 2):
        even, odd = spin_rows(stage_hi[rows], stage_lo[rows], table, 2)
        spec[rows, 0 * PART : 1 * PART] = even[:, :PART] + odd[:, :PART]
        spec[rows, 1 * PART : 2 * PART] = even[:, :PART] - odd[:, :PART]
        spec[rows, 2 * PART : 3 * PART] = even[:, PART:] + odd[:, PART:]
        spec[rows, 3 * PART : 4 * PART] = even[:, PART:] - odd[:, PART:]
    cos, sin = twiddle[0], twiddle[1]
    first = lax.broadcasted_iota(jnp.int32, (8, WIDTH), 0) == 0
    ends = spec[base:size]
    ends = ends[:, :WIDTH] * twiddle[3, 0:1] + ends[:, WIDTH:] * twiddle[3, 1:2]
    for pair in range(count // 2):
        sides = []
        for k in range(2):
            n = pair * 2 + k
            piece = spec[n * HALF : (n + 1) * HALF]
            re, im = piece[:, :WIDTH], piece[:, WIDTH:]
            im, re = im * cos - re * sin, re * cos + im * sin
            top = jnp.where(first, jnp.broadcast_to(ends[n : n + 1], (8, WIDTH)), im[:8])
            sides.append(jnp.concatenate([re, top, im[8:]], 0))
        high, low = split(jnp.concatenate(sides, 1))
        store(pair * 2, dot(back[...], jnp.concatenate([high, high, low], 0)))


def store_pair(ref, first, value):
    for k in range(4):
        n = first + k // 2
        ref[pl.ds(row_of(n, k % 2, 5), ACROSS, stride=40), :] = value[:, k * 128 : (k + 1) * 128]


def grads_kernel(got, across, back, twiddle, table, out, spec, stage_hi, stage_lo, ends, extra):
    load = functools.partial(load_pair, got)
    spectra_of(load, 36, across, twiddle, table, stage_hi, stage_lo, ends, spec)
    for tail in (False, True):

        def take(n):
            rows = spec[36 * HALF + n : 36 * HALF + n + 1] if tail else spec[n * HALF : (n + 1) * HALF]
            return rows[:, :WIDTH], rows[:, WIDTH:]

        def put(n, re, im):
            rows = jnp.concatenate([re, im], 1)
            if tail:
                extra[n : n + 1] = rows
            else:
                high, low = split(rows)
                stage_hi[n * HALF : (n + 1) * HALF] = high
                stage_lo[n * HALF : (n + 1) * HALF] = low

        crosses = []
        for s in range(4):
            own, other = take(16 + s), take(19 - s)
            er, ei = own[0] + other[0], own[1] - other[1]
            re = im = 0.0
            for b in range(4):
                n = b * 4 + s
                (cr, ci), (xr, xi) = take(n), take(20 + n)
                put(n, er * cr + ei * ci, ei * cr - er * ci)
                re = re + (cr * xr + ci * xi)
                im = im + (cr * xi - ci * xr)
            crosses.append((re, im))
        for s in range(4):
            a, b = crosses[s], crosses[3 - s]
            put(16 + s, a[0] + b[0], a[1] - b[1])
    high, low = split(extra[...])
    stage_hi[20 * HALF : 20 * HALF + 32] = high
    stage_lo[20 * HALF : 20 * HALF + 32] = low
    positions_of(
        20, back, twiddle, table, stage_hi, stage_lo, spec, functools.partial(store_pair, out)
    )


def call(kernel, outs, scratch, flops, *args, in_specs=None, out_specs=None, vmem=VMEM, near=False):
    moved = sum(a.size * a.dtype.itemsize for a in args) + sum(4 * math.prod(o) for o in outs)
    options = dict(in_specs=in_specs) if in_specs else {}
    if out_specs:
        options["out_specs"] = out_specs
    return pl.pallas_call(
        kernel,
        out_shape=[(pltpu.VMEM if near else jax.ShapeDtypeStruct)(o, F32) for o in outs],
        scratch_shapes=scratch,
        compiler_params=pltpu.CompilerParams(vmem_limit_bytes=vmem),
        cost_estimate=pl.CostEstimate(flops=flops, bytes_accessed=moved, transcendentals=0),
        **options,
    )(*args)


def exchange(value, units):
    groups = [[i * 4 + s for i in range(ACROSS) for s in (low, 3 - low)] for low in range(2)]
    blocks = value.reshape(GROUP, units, 4, 128)
    return lax.all_to_all(
        blocks, ("ctx", "ch"), 0, 0, axis_index_groups=groups, tiled=True
    ).reshape(-1, 128)


def body(inputs, cotangent, filters):
    across, back, twiddle, table = [jnp.asarray(t) for t in tables()]
    far = pl.BlockSpec(memory_space=pltpu.HBM)
    (packed,) = call(
        pack_kernel,
        [(GROUP * 36, 128)],
        [pltpu.VMEM((9, WIDTH, WIDTH), F32), pltpu.SemaphoreType.DMA((5,))],
        10**9,
        cotangent, filters, inputs,
        in_specs=[far] * 3,
        vmem=PACK_VMEM,
        near=True,
    )
    got = exchange(packed, 9)
    (grads,) = call(
        grads_kernel,
        [(GROUP * 20, 128)],
        [pltpu.VMEM((36 * HALF + 48, 2 * WIDTH), F32)]
        + [pltpu.VMEM((36 * HALF + 48, 2 * WIDTH), BF)] * 2
        + [pltpu.VMEM((48, WIDTH), F32), pltpu.VMEM((32, 2 * WIDTH), F32)],
        8 * 10**9,
        got, across, back, twiddle, table,
    )
    return tuple(
        call(
            unpack_kernel,
            [(4, WIDTH, WIDTH), (WIDTH, WIDTH)],
            [pltpu.VMEM((5, WIDTH, WIDTH), F32), pltpu.SemaphoreType.DMA((5,))],
            10**9,
            exchange(grads, 5),
            out_specs=[far] * 2,
        )
    )


def solution(mesh):
    in_specs = (P(None, "ctx", "ch"), P(None, "ctx", "ch"), P("ctx", "ch"))
    out_specs = (P(None, "ctx", "ch"), P("ctx", "ch"))
    return jax.shard_map(body, mesh=mesh, in_specs=in_specs, out_specs=out_specs, check_vma=False)
```

```python
import functools
import math

import jax
import jax.numpy as jnp
import numpy as np
from jax import lax
from jax.experimental import pallas as pl
from jax.experimental.pallas import tpu as pltpu
from jax.sharding import PartitionSpec as P

BF = jnp.bfloat16
F32 = jnp.float32
ACROSS = 64
GROUP = 2 * ACROSS
WIDTH = 256
PART = WIDTH // 2
PERIOD = ACROSS * WIDTH
HALF = ACROSS // 2
FACTOR = 1.0 / (PERIOD * math.sqrt(2.0 * PERIOD))
VMEM = 48 * 1024 * 1024
PACK_VMEM = 56 * 1024 * 1024


def two_parts(table):
    high = np.asarray(table, np.float32).astype(jnp.bfloat16)
    low = (table - high.astype(np.float64)).astype(np.float32).astype(jnp.bfloat16)
    return high, low


def tables():
    p = np.arange(HALF)
    i = np.arange(ACROSS)
    angle = 2.0 * np.pi * (np.outer(p, i) % ACROSS) / ACROSS
    cos, sin = np.cos(angle), np.sin(angle)
    last = np.cos(np.pi * i)
    fore = np.concatenate([cos, -sin], 0)
    fore[HALF] = last
    high, low = two_parts(fore)
    across = np.concatenate([high, low, high], 1)
    weight = np.where(p == 0, 1.0, 2.0)[:, None] * FACTOR
    back = np.concatenate([cos * weight, sin * weight], 0)
    back[HALF] = last * FACTOR
    high, low = two_parts(back.T)
    back = np.concatenate([high, low, high], 1)
    j = np.arange(WIDTH)
    turn = 2.0 * np.pi * np.outer(np.arange(HALF + 1), j) / PERIOD
    c, s = np.cos(turn), np.sin(turn)
    masked = c[:HALF] * (p > 0)[:, None]
    ends = np.zeros((HALF, WIDTH))
    ends[0], ends[1] = c[HALF], s[HALF]
    twiddle = np.stack([c[:HALF], s[:HALF], masked, ends]).astype(np.float32)
    j = np.arange(PART)
    parts = []
    for turns in (2 * np.outer(j, j), np.outer(j, 2 * j + 1), np.outer(2 * j + 1, j)):
        spin = 2.0 * np.pi * (turns % WIDTH) / WIDTH
        c, s = np.cos(spin), np.sin(spin)
        high, low = two_parts(np.block([[c, -s], [s, c]]))
        parts.append(np.concatenate([high, high, low], 0))
    return across, back, twiddle, np.stack(parts)


def split(value):
    high = value.astype(BF)
    return high, (value - high.astype(F32)).astype(BF)


def dot(left, right):
    return jnp.dot(left, right, preferred_element_type=F32)


def mirrored(value):
    back = 7 - lax.broadcasted_iota(jnp.int32, (8, 128), 0)
    columns = []
    for half in range(2):
        lanes = slice(half * 128, (half + 1) * 128)
        groups = [value[k * 8 : (k + 1) * 8, lanes] for k in reversed(range(value.shape[0] // 8))]
        columns.append(
            jnp.concatenate([jnp.take_along_axis(group, back, axis=0) for group in groups], 0)
        )
    return jnp.concatenate(columns, 1)


def both_halves(run):
    upper = lax.axis_index("ch") >= 2
    pl.when(upper)(functools.partial(run, mirrored))
    pl.when(jnp.logical_not(upper))(functools.partial(run, lambda value: value))


def pack_kernel(cotangent, filters, inputs, out, held, sems):
    pieces = [((4,), filters, held.at[4])]
    for base, source in ((0, cotangent), (5, inputs)):
        units = tuple(range(base, base + 4))
        pieces.append((units, source, held.at[pl.ds(base, 4)]))
    copies = [
        pltpu.make_async_copy(source, target, sems.at[k])
        for k, (_, source, target) in enumerate(pieces)
    ]
    for copy in copies:
        copy.start()

    def run(order):
        for copy, (units, _, _) in zip(copies, pieces):
            copy.wait()
            for u in units:
                turned = order(held[u].T)
                for k in range(4):
                    out[pl.ds(u * 4 + k, GROUP, stride=36), :] = turned[
                        k // 2 * GROUP : (k // 2 + 1) * GROUP, k % 2 * 128 : (k % 2 + 1) * 128
                    ]

    both_halves(run)


def unpack_kernel(ref, inputs, filters, held, sems):
    blocks = [inputs.at[b] for b in range(4)] + [filters]
    copies = [pltpu.make_async_copy(held.at[u], block, sems.at[u]) for u, block in enumerate(blocks)]

    def run(order):
        for u, copy in enumerate(copies):
            parts = [ref[pl.ds(u * 4 + k, GROUP, stride=20), :] for k in range(4)]
            sides = [jnp.concatenate(parts[k : k + 2], 1) for k in (0, 2)]
            held[u] = order(jnp.concatenate(sides, 0)).T
            copy.start()
        for copy in copies:
            copy.wait()

    both_halves(run)


def row_of(n, half, units):
    side, slot = ((0, 0), (0, 1), (1, 1), (1, 0))[n % 4]
    return ((side * units + n // 4) * 2 + slot) * 2 + half


def load_pair(ref, first):
    pieces = []
    for n in (first, first + 1):
        for half in range(2):
            pieces.append(ref[pl.ds(row_of(n, half, 9), ACROSS, stride=72), :])
    return jnp.concatenate(pieces, 1)


def spin_rows(high, low, table, odd):
    results = []
    for k, which in enumerate((0, odd)):
        h = jnp.concatenate([high[:, k * PART : (k + 1) * PART], high[:, (k + 2) * PART : (k + 3) * PART]], 1)
        l = jnp.concatenate([low[:, k * PART : (k + 1) * PART], low[:, (k + 2) * PART : (k + 3) * PART]], 1)
        results.append(dot(jnp.concatenate([h, l, h], 1), table[which]))
    return results


def shares(size, parts):
    step = size // parts
    return [slice(at, at + step) for at in range(0, size, step)]


def butterfly(value):
    a, b = value[:, :PART], value[:, PART:]
    return [a + b, a - b]


def spectra_of(load, count, across, twiddle, table, stage_hi, stage_lo, ends, spec):
    cos, sin, masked = twiddle[0], twiddle[1], twiddle[2]
    for pair in range(count // 2):
        high, low = split(load(pair * 2))
        part = dot(across[...], jnp.concatenate([high, high, low], 0))
        turned = []
        for k in range(2):
            re = part[:HALF, k * WIDTH : (k + 1) * WIDTH]
            im = part[HALF:, k * WIDTH : (k + 1) * WIDTH]
            ends[pair * 2 + k : pair * 2 + k + 1, :] = im[:1]
            re, im = re * cos + im * sin, im * masked - re * sin
            turned.append(jnp.concatenate(butterfly(re) + butterfly(im), 1))
        high, low = split(jnp.concatenate(turned, 0))
        stage_hi[pair * 64 : pair * 64 + 64] = high
        stage_lo[pair * 64 : pair * 64 + 64] = low
    base, more = count * HALF, ends.shape[0]
    last = ends[...]
    pieces = butterfly(last * twiddle[3, 0:1]) + butterfly(-last * twiddle[3, 1:2])
    high, low = split(jnp.concatenate(pieces, 1))
    stage_hi[base : base + more] = high
    stage_lo[base : base + more] = low
    for rows in shares(base + more, 3):
        even, odd = spin_rows(stage_hi[rows], stage_lo[rows], table, 1)
        spec[rows, 0 * PART : 1 * PART] = even[:, :PART]
        spec[rows, 1 * PART : 2 * PART] = odd[:, :PART]
        spec[rows, 2 * PART : 3 * PART] = even[:, PART:]
        spec[rows, 3 * PART : 4 * PART] = odd[:, PART:]


def positions_of(count, back, twiddle, table, stage_hi, stage_lo, spec, store):
    base = count * HALF
    size = base + 32
    for rows in shares(size, 2):
        even, odd = spin_rows(stage_hi[rows], stage_lo[rows], table, 2)
        spec[rows, 0 * PART : 1 * PART] = even[:, :PART] + odd[:, :PART]
        spec[rows, 1 * PART : 2 * PART] = even[:, :PART] - odd[:, :PART]
        spec[rows, 2 * PART : 3 * PART] = even[:, PART:] + odd[:, PART:]
        spec[rows, 3 * PART : 4 * PART] = even[:, PART:] - odd[:, PART:]
    cos, sin = twiddle[0], twiddle[1]
    first = lax.broadcasted_iota(jnp.int32, (8, WIDTH), 0) == 0
    ends = spec[base:size]
    ends = ends[:, :WIDTH] * twiddle[3, 0:1] + ends[:, WIDTH:] * twiddle[3, 1:2]
    for pair in range(count // 2):
        sides = []
        for k in range(2):
            n = pair * 2 + k
            piece = spec[n * HALF : (n + 1) * HALF]
            re, im = piece[:, :WIDTH], piece[:, WIDTH:]
            im, re = im * cos - re * sin, re * cos + im * sin
            top = jnp.where(first, jnp.broadcast_to(ends[n : n + 1], (8, WIDTH)), im[:8])
            sides.append(jnp.concatenate([re, top, im[8:]], 0))
        high, low = split(jnp.concatenate(sides, 1))
        store(pair * 2, dot(back[...], jnp.concatenate([high, high, low], 0)))


def store_pair(ref, first, value):
    for k in range(4):
        n = first + k // 2
        ref[pl.ds(row_of(n, k % 2, 5), ACROSS, stride=40), :] = value[:, k * 128 : (k + 1) * 128]


def grads_kernel(got, across, back, twiddle, table, out, spec, stage_hi, stage_lo, ends, extra):
    load = functools.partial(load_pair, got)
    spectra_of(load, 36, across, twiddle, table, stage_hi, stage_lo, ends, spec)
    for tail in (False, True):

        def take(n):
            rows = spec[36 * HALF + n : 36 * HALF + n + 1] if tail else spec[n * HALF : (n + 1) * HALF]
            return rows[:, :WIDTH], rows[:, WIDTH:]

        def put(n, re, im):
            rows = jnp.concatenate([re, im], 1)
            if tail:
                extra[n : n + 1] = rows
            else:
                high, low = split(rows)
                stage_hi[n * HALF : (n + 1) * HALF] = high
                stage_lo[n * HALF : (n + 1) * HALF] = low

        crosses = []
        for s in range(4):
            own, other = take(16 + s), take(19 - s)
            er, ei = own[0] + other[0], own[1] - other[1]
            re = im = 0.0
            for b in range(4):
                n = b * 4 + s
                (cr, ci), (xr, xi) = take(n), take(20 + n)
                put(n, er * cr + ei * ci, ei * cr - er * ci)
                re = re + (cr * xr + ci * xi)
                im = im + (cr * xi - ci * xr)
            crosses.append((re, im))
        for s in range(4):
            a, b = crosses[s], crosses[3 - s]
            put(16 + s, a[0] + b[0], a[1] - b[1])
    high, low = split(extra[...])
    stage_hi[20 * HALF : 20 * HALF + 32] = high
    stage_lo[20 * HALF : 20 * HALF + 32] = low
    positions_of(
        20, back, twiddle, table, stage_hi, stage_lo, spec, functools.partial(store_pair, out)
    )


def call(kernel, outs, scratch, flops, *args, in_specs=None, out_specs=None, vmem=VMEM, near=False):
    moved = sum(a.size * a.dtype.itemsize for a in args) + sum(4 * math.prod(o) for o in outs)
    options = dict(in_specs=in_specs) if in_specs else {}
    if out_specs:
        options["out_specs"] = out_specs
    return pl.pallas_call(
        kernel,
        out_shape=[(pltpu.VMEM if near else jax.ShapeDtypeStruct)(o, F32) for o in outs],
        scratch_shapes=scratch,
        compiler_params=pltpu.CompilerParams(vmem_limit_bytes=vmem),
        cost_estimate=pl.CostEstimate(flops=flops, bytes_accessed=moved, transcendentals=0),
        **options,
    )(*args)


def exchange(value, units):
    groups = [[i * 4 + s for i in range(ACROSS) for s in (low, 3 - low)] for low in range(2)]
    blocks = value.reshape(GROUP, units, 4, 128)
    return lax.all_to_all(
        blocks, ("ctx", "ch"), 0, 0, axis_index_groups=groups, tiled=True
    ).reshape(-1, 128)


def body(inputs, cotangent, filters):
    across, back, twiddle, table = [jnp.asarray(t) for t in tables()]
    far = pl.BlockSpec(memory_space=pltpu.HBM)
    (packed,) = call(
        pack_kernel,
        [(GROUP * 36, 128)],
        [pltpu.VMEM((9, WIDTH, WIDTH), F32), pltpu.SemaphoreType.DMA((3,))],
        10**9,
        cotangent, filters, inputs,
        in_specs=[far] * 3,
        vmem=PACK_VMEM,
        near=True,
    )
    got = exchange(packed, 9)
    (grads,) = call(
        grads_kernel,
        [(GROUP * 20, 128)],
        [pltpu.VMEM((36 * HALF + 48, 2 * WIDTH), F32)]
        + [pltpu.VMEM((36 * HALF + 48, 2 * WIDTH), BF)] * 2
        + [pltpu.VMEM((48, WIDTH), F32), pltpu.VMEM((32, 2 * WIDTH), F32)],
        8 * 10**9,
        got, across, back, twiddle, table,
    )
    return tuple(
        call(
            unpack_kernel,
            [(4, WIDTH, WIDTH), (WIDTH, WIDTH)],
            [pltpu.VMEM((5, WIDTH, WIDTH), F32), pltpu.SemaphoreType.DMA((5,))],
            10**9,
            exchange(grads, 5),
            out_specs=[far] * 2,
        )
    )


def solution(mesh):
    in_specs = (P(None, "ctx", "ch"), P(None, "ctx", "ch"), P("ctx", "ch"))
    out_specs = (P(None, "ctx", "ch"), P("ctx", "ch"))
    return jax.shard_map(body, mesh=mesh, in_specs=in_specs, out_specs=out_specs, check_vma=False)
```
